256 devices in a mesh: band: 8 (over x, y_lo), fft: 32 (over z, y_hi, core).
Axes of the slice: x: 4, y: 4 (y_hi: 2, y_lo: 2; y = y_hi * 2 + y_lo), z: 8, core: 2. Of those that a mesh axis runs over, the one named last changes fastest.
Arguments:
- orbitals: float32 [8, 256, 256, 256], P('band', 'fft'), may hold values from -6 to 6
- band_ids: int32 [8], replicated, may hold values from 0 to 7, each once
- owners: int32 [2], replicated, may hold values from 0 to 7, as said below
Outputs:
- exchange_potential: float32 [8, 256, 256, 256], P('band', 'fft')
The draws below stay inside these ranges and needn't reach their ends.
Inputs may be any that keep to these rules, and one draw needn't show every extreme that they name: `band_ids`: each band number stands in exactly one slot; slot s belongs to band group s. `owners`: 2 different band numbers, one of which is 7.
All inputs are finite; a program needn't handle non-finite values.
Results may differ from the reference program's by a relative error of at most 0.0003.
Values sent between devices are 32-bit elements; how exact they have to be, the bound alone decides.
A program may use at most 64 MiB of HBM per device.

```python
import math
import jax
import jax.numpy as jnp
from jax import lax

NG = 256
OWN = 2
BANDS = 8


def draw_owners(key, part):
    key = jax.random.fold_in(key, 7)
    score_key = jax.random.fold_in(key, 1)
    place_key = jax.random.fold_in(key, 2)
    scores = jax.random.randint(score_key, (BANDS - 1,), 0, 1 << 20, dtype=jnp.int32)
    scores = scores * BANDS + jnp.arange(BANDS - 1, dtype=jnp.int32)
    others = jax.lax.top_k(scores, OWN - 1)[1].astype(jnp.int32)
    chosen = jnp.concatenate([jnp.full((1,), BANDS - 1, dtype=jnp.int32), others])
    offset = jax.random.randint(place_key, (), 0, OWN, dtype=jnp.int32)
    return jnp.roll(chosen, offset).astype(jnp.int32)


def block_levels(rng, extent, pieces, least, top_value):
    level, own = 1.0, jax.random.fold_in(rng, 6)
    for axis_at, blocks in pieces:
        heights = jnp.exp(jax.random.uniform(jax.random.fold_in(own, axis_at), (blocks,), jnp.float32, least / len(pieces), top_value / len(pieces)))
        level = level * jnp.repeat(heights, extent[axis_at] // blocks).reshape([-1 if axis == axis_at else 1 for axis in range(len(extent))])
    return level


def normal_values(own_key, shape, width, limit, split=(), kind=jnp.bfloat16):
    loudness = block_levels(own_key, shape, split, -0.22, 0.18) if split else 1.0
    array = jax.random.normal(own_key, shape, jnp.float32) * width * loudness
    return jnp.minimum(jnp.maximum(array, -limit), limit).astype(kind)


def setup_inputs(seed: int = 0) -> dict:
    splits = jax.random.split(jax.random.key(seed), 4)
    return {
        "orbitals": normal_values(splits[0], (BANDS, NG, NG, NG), 1.0, 6.0, ((0, 8), (1, 32)), jnp.float32),
        "band_ids": jax.random.permutation(splits[1], BANDS).astype(jnp.int32),
        "owners": draw_owners(jax.random.fold_in(splits[3], 71), 0),
    }


cell_length = 46.9


def coulomb(points):
    freq_list = jnp.arange(points, dtype=jnp.int32)
    wave = jnp.where(freq_list < points // 2, freq_list, freq_list - points).astype(jnp.int32)
    square_sum = wave[:, None, None] ** 2 + wave[None, :, None] ** 2 + wave[None, None, :] ** 2
    inside = (square_sum > 0) & (square_sum < (points // 4) ** 2)
    safe_sum = jnp.where(inside, square_sum, 1).astype(jnp.float32)
    return jnp.where(inside, (cell_length ** 2 / math.pi) / safe_sum, jnp.float32(0.0))


def reference(orbitals, band_ids, owners):
    matches = band_ids[:, None] == owners[None, :]
    slot_ids = jnp.sum(jnp.where(matches, jnp.arange(BANDS, dtype=jnp.int32)[:, None], 0), axis=0).astype(jnp.int32)
    owner_orbitals = jnp.take(orbitals, slot_ids, axis=0)
    kernel = coulomb(NG)

    def potential(orbital):
        total = jnp.zeros(orbital.shape, jnp.float32)
        for owner_index in range(OWN):
            density = owner_orbitals[owner_index] * orbital
            spectrum = jnp.fft.fftn(density)
            field = jnp.real(jnp.fft.ifftn(kernel * spectrum))
            total = total - owner_orbitals[owner_index] * field
        return total

    return lax.map(potential, orbitals)
```

```python
import math

import jax
import jax.numpy as jnp
from jax import lax
from jax.sharding import PartitionSpec as P

cell_length = 46.9
highest = lax.Precision.HIGHEST


def broadcast(value, axis, source):
    kept = jnp.where(lax.axis_index(axis) == source, value, 0).astype(value.dtype)
    return lax.psum(kept, axis)


def cas_matrix(points, freq_list):
    positions = jnp.arange(points, dtype=jnp.int32)
    product = positions[:, None] * freq_list[None, :] % points
    angles = product.astype(jnp.float32) * (2.0 * math.pi / points)
    return jnp.cos(angles) + jnp.sin(angles)


def centred(freq_list, points):
    return jnp.where(freq_list < points // 2, freq_list, freq_list - points)


def coulomb_block(freq_x, freq_y, freq_z, points):
    wave_x = centred(freq_x, points)
    wave_y = centred(freq_y, points)
    wave_z = centred(freq_z, points)
    square_sum = (
        wave_x[:, None, None] ** 2 + wave_y[None, :, None] ** 2 + wave_z[None, None, :] ** 2
    )
    inside = (square_sum > 0) & (square_sum < (points // 4) ** 2)
    safe_sum = jnp.where(inside, square_sum, 1).astype(jnp.float32)
    weights = jnp.where(inside, cell_length**2 / math.pi / safe_sum, jnp.float32(0.0))
    return weights / float(points) ** 3


def per_device(orbitals, band_ids, owners):
    slot_count = orbitals.shape[0]
    planes = orbitals.shape[1]
    points = orbitals.shape[2]
    owner_count = owners.shape[0]
    all_slots = band_ids.shape[0]
    matches = band_ids[:, None] == owners[None, :]
    slot_ids = jnp.sum(
        jnp.where(matches, jnp.arange(all_slots, dtype=jnp.int32)[:, None], 0), axis=0
    )
    root_ids = slot_ids // slot_count
    local_slots = slot_ids % slot_count
    picked = jnp.take(orbitals, local_slots, axis=0)
    shared = []
    for owner_index in range(owner_count):
        shared.append(broadcast(picked[owner_index], "band", root_ids[owner_index]))
    owner_orbitals = jnp.stack(shared)
    density = (owner_orbitals[:, None] * orbitals[None, :]).reshape(
        owner_count * slot_count, planes, points, points
    )
    freq_list = jnp.arange(points, dtype=jnp.int32)
    half = points // 2
    freq_list = (freq_list[:half] - half // 2) % points
    cas_rows = cas_matrix(points, freq_list)
    spectrum = jnp.einsum("pxyz,zk->pxyk", density, cas_rows, precision=highest)
    spectrum = jnp.einsum("pxyk,yj->pxjk", spectrum, cas_rows, precision=highest)
    column_count = freq_list.shape[0] // lax.axis_size("fft")
    first_col = lax.axis_index("fft") * column_count
    freq_cols = lax.dynamic_slice_in_dim(freq_list, first_col, column_count)
    kernel = coulomb_block(freq_list, freq_cols, freq_list, points)
    coeffs = jnp.einsum(
        "pxjk,xi->pijk",
        lax.all_to_all(spectrum, "fft", split_axis=2, concat_axis=1, tiled=True),
        cas_rows,
        precision=highest,
    )
    coeffs = coeffs * kernel[None]
    restored = jnp.einsum("pijk,xi->pxjk", coeffs, cas_rows, precision=highest)
    returned = lax.all_to_all(restored, "fft", split_axis=1, concat_axis=2, tiled=True)
    potential = jnp.einsum("pxjk,yj->pxyk", returned, cas_rows, precision=highest)
    potential = jnp.einsum("pxyk,zk->pxyz", potential, cas_rows, precision=highest)
    potential = potential.reshape(owner_count, slot_count, planes, points, points)
    return -jnp.sum(owner_orbitals[:, None] * potential, axis=0)


def solution(mesh):
    placed = (P("band", "fft", None, None), P(), P())
    return jax.shard_map(
        per_device,
        mesh=mesh,
        in_specs=placed,
        out_specs=P("band", "fft", None, None),
        check_vma=False,
    )
```

```python
import functools
import itertools
import math

import jax
import jax.numpy as jnp
import ml_dtypes
import numpy as np
from jax import lax
from jax.experimental import pallas as pl
from jax.experimental.pallas import tpu as pltpu
from jax.sharding import PartitionSpec as P

MESH = pl.DeviceIdType.MESH
F32 = jnp.float32
BF16 = jnp.bfloat16
cell_length = 46.9

POINTS = 256
FREQS = 128
PLANES = 8
CHIPS = 16
GROUP = 2
VMEM_MIB = 60
PIECES = 1
ROWS = ((0, 88), (88, 88), (176, 80))
SLACK = 2
LAG = 3
TREES = (
    ((0, 2, 4, 5), (3,), (2, 4)),
    ((7,), (0, 6, 4, 7, 5), (6,)),
    ((1, 3), (1,), (0, 3, 5, 7)),
)
DEPTHS = ((0, 3, 1, 2, 2, 3, 3, 4), (0, 3, 3, 4, 2, 3, 1, 2), (0, 1, 3, 2, 4, 3, 3, 2))


def split(value):
    high = value.astype(BF16)
    return high, (value - high.astype(F32)).astype(BF16)


def dot(left, right):
    return jnp.dot(left, right, preferred_element_type=F32)


def quarters(value):
    rows, columns = value.shape[0] // 2, value.shape[1] // 2
    small = (value[:rows, columns:] + value[rows:, :columns]) + value[rows:, columns:]
    return value[:rows, :columns] + small


def kernel(
    roots, orb_ref, tall_in, wide_in, out_ref,
    tall_ref, wide_ref, held, own, ahead, arrived, back, restored, weights, partial, result,
    in_sem, tree_send, tree_recv, ahead_send, ahead_recv, back_send, back_recv, out_sem,
):
    band = lax.axis_index("band")
    place = lax.axis_index("fft")
    my_x, my_y = band // 2, band % 2
    chip, core = place // 2, place % 2
    neighbours = (((my_x + 1) % 4) * 2 + my_y, ((my_x + 3) % 4) * 2 + my_y, my_x * 2 + (my_y + 1) % 2)

    load = pltpu.make_async_copy(orb_ref.at[0], own, in_sem.at[0])
    load.start()
    tables = (
        pltpu.make_async_copy(tall_in, tall_ref, in_sem.at[3]),
        pltpu.make_async_copy(wide_in, wide_ref, in_sem.at[4]),
    )
    for table in tables:
        table.start()
    for o in range(2):
        @pl.when(band == roots[o])
        def _():
            pltpu.make_async_copy(orb_ref.at[0], held.at[o], in_sem.at[1 + o]).start()

    barrier = pltpu.get_barrier_semaphore()
    for other in neighbours:
        pl.semaphore_signal(barrier, inc=1, device_id=(other, place), device_id_type=MESH)

    def greet(k, _):
        pl.semaphore_signal(
            barrier, inc=1, device_id=(band, (place + k) % 32), device_id_type=MESH
        )
        return 0

    lax.fori_loop(1, 32, greet, 0)

    kx = lax.broadcasted_iota(jnp.int32, (FREQS, FREQS), 0) - FREQS // 2
    kz = lax.broadcasted_iota(jnp.int32, (FREQS, FREQS), 1) - FREQS // 2

    def weigh(row, _):
        ky = chip * 8 + row - FREQS // 2
        square = kx * kx + kz * kz + ky * ky
        inside = (square > 0) & (square < FREQS * FREQS // 4)
        safe = jnp.where(inside, square, 1).astype(F32)
        scale = cell_length**2 / math.pi / float(POINTS) ** 3
        weights[row] = jnp.where(inside, jnp.float32(scale) / safe, jnp.float32(0.0))
        return 0

    lax.fori_loop(0, 8, weigh, 0)

    load.wait()
    for table in tables:
        table.wait()
    for o in range(2):
        @pl.when(band == roots[o])
        def _():
            pltpu.make_async_copy(orb_ref.at[0], held.at[o], in_sem.at[1 + o]).wait()
    pl.semaphore_wait(barrier, 34)

    def relation(o):
        root = roots[o]
        return ((my_x - root // 2 + 4) % 4) * 2 + (my_y + root) % 2

    def flag(relative, members):
        found = relative == members[0]
        for member in members[1:]:
            found = found | (relative == member)
        return found

    relatives = [relation(o) for o in range(2)]
    depths = [
        [SLACK * sum(jnp.where(relatives[o] == k, d, 0) for k, d in enumerate(DEPTHS[i])) for i in range(3)]
        for o in range(2)
    ]
    flags = [
        [[flag(relatives[o], TREES[i][way]) for way in range(3)] for i in range(3)]
        for o in range(2)
    ]

    def relay(turn):
        for o in range(2):
            for i, (first, count) in enumerate(ROWS):
                chunk = turn - depths[o][i] - PLANES * PIECES * o

                @pl.when((chunk >= 0) & (chunk < PLANES * PIECES))
                def _():
                    at = jnp.clip(chunk, 0, PLANES * PIECES - 1)
                    p, piece = at // PIECES, at % PIECES
                    start = pl.multiple_of(piece * (POINTS // PIECES) + first, 8)
                    part = held.at[o, p, pl.ds(start, count)]

                    @pl.when(relatives[o] != 0)
                    def _():
                        pltpu.make_async_copy(part, part, tree_recv.at[o, at, i]).wait()

                    for way in range(3):
                        @pl.when(flags[o][i][way])
                        def _():
                            pltpu.make_async_remote_copy(
                                src_ref=part, dst_ref=part,
                                send_sem=tree_send.at[o, i, way],
                                recv_sem=tree_recv.at[o, at, i],
                                device_id=(neighbours[way], place), device_id_type=MESH,
                            ).start()

    def forward(o, p):
        density = held[o, p] * own[p]
        level = jnp.sum(density, keepdims=True) * (1.0 / POINTS**2)
        high, low = split(density - level)
        along_z = quarters(dot(jnp.concatenate([high, low], axis=0), tall_ref[...]))
        high, low = split(along_z)
        along_y = quarters(dot(wide_ref[...], jnp.concatenate([high, low], axis=1)))
        along_y = along_y + jnp.where((kx == 0) & (kz == 0), level * float(POINTS**2), 0.0)
        ahead[o, :, p] = along_y.reshape(CHIPS, 8, FREQS)

    def send_ahead(o, p):
        first = (p // GROUP) * GROUP

        def one(k, _):
            there = (chip + k) % CHIPS
            source = ahead.at[o, there, pl.ds(first, GROUP)]
            target = arrived.at[pl.ds(place * PLANES + first, GROUP)]
            here = there * 2 + o == place

            @pl.when(here)
            def _():
                pltpu.make_async_copy(source, target, ahead_recv.at[0]).start()

            @pl.when(jnp.logical_not(here))
            def _():
                pltpu.make_async_remote_copy(
                    src_ref=source, dst_ref=target,
                    send_sem=ahead_send.at[o], recv_sem=ahead_recv.at[0],
                    device_id=(band, there * 2 + o), device_id_type=MESH,
                ).start()

            return 0

        lax.fori_loop(0, CHIPS, one, 0)

    def step(turn, _):
        relay(turn)
        done = turn - 4 * SLACK

        @pl.when((done >= 0) & (done % PIECES == PIECES - 1))
        def _():
            q = jnp.maximum(done, 0) // PIECES
            o, p = q // PLANES, q % PLANES
            forward(o, p)

            @pl.when(p % GROUP == GROUP - 1)
            def _():
                send_ahead(o, p)

        return 0

    half = PLANES // 2

    def middle(o):
        @pl.when(core == o)
        def _():
            pltpu.make_async_copy(arrived, arrived, ahead_recv.at[0]).wait()

            def one(row, _):
                column = arrived[:, pl.ds(row, 1), :].reshape(POINTS, FREQS)
                level = jnp.sum(column, axis=0, keepdims=True) * (1.0 / POINTS)
                high, low = split(column - level)
                along_x = quarters(dot(wide_ref[...], jnp.concatenate([high, low], axis=1)))
                along_x = along_x + jnp.where(kx == 0, level * float(POINTS), 0.0)
                high, low = split(along_x * weights[row])
                pair = jnp.concatenate([high, low], axis=1)
                both = dot(tall_ref[...], jnp.concatenate([pair, pair], axis=0))
                back[:, pl.ds(row, 1), :] = (both[:, :FREQS] + both[:, FREQS:]).reshape(POINTS, 1, FREQS)
                return 0

            lax.fori_loop(0, 8, one, 0, unroll=True)
            for h in range(2):
                def one(k, _):
                    there = (place + k) % 32
                    source = back.at[pl.ds(there * PLANES + h * half, half)]
                    target = restored.at[o, chip, pl.ds(h * half, half)]

                    @pl.when(k == 0)
                    def _():
                        pltpu.make_async_copy(source, target, back_recv.at[o, h]).start()

                    @pl.when(k != 0)
                    def _():
                        pltpu.make_async_remote_copy(
                            src_ref=source, dst_ref=target,
                            send_sem=back_send.at[0], recv_sem=back_recv.at[o, h],
                            device_id=(band, there), device_id_type=MESH,
                        ).start()

                    return 0

                lax.fori_loop(0, 32, one, 0)

    def backward(o, p):
        high, low = split(restored[o, :, p].reshape(FREQS, FREQS))
        pair = jnp.concatenate([high, low], axis=1)
        both = dot(tall_ref[...], jnp.concatenate([pair, pair], axis=0))
        high, low = split(both[:, :FREQS] + both[:, FREQS:])
        field = dot(jnp.concatenate([high, low], axis=1), jnp.concatenate([wide_ref[:FREQS], wide_ref[:FREQS]], axis=0))
        field = field + dot(high, wide_ref[FREQS:])
        return held[o, p] * field

    turns = 2 * PLANES * PIECES + 4 * SLACK
    pause = turns - (PLANES - LAG) * PIECES
    lax.fori_loop(0, pause, step, 0)
    middle(0)
    lax.fori_loop(pause, turns, step, 0)
    middle(1)

    for h in range(2):
        part = restored.at[0, :, pl.ds(h * half, half)]
        pltpu.make_async_copy(part, part, back_recv.at[0, h]).wait()

        def one(p, _):
            partial[p] = backward(0, p)
            return 0

        lax.fori_loop(h * half, (h + 1) * half, one, 0)
    for h in range(2):
        part = restored.at[1, :, pl.ds(h * half, half)]
        pltpu.make_async_copy(part, part, back_recv.at[1, h]).wait()

        def one(p, _):
            result[p] = -(partial[p] + backward(1, p))
            return 0

        lax.fori_loop(h * half, (h + 1) * half, one, 0)
        pltpu.make_async_copy(
            result.at[pl.ds(h * half, half)], out_ref.at[0, pl.ds(h * half, half)], out_sem.at[h]
        ).start()

    for o in range(2):
        for i, (first, count) in enumerate(ROWS):
            part = held.at[o, :, pl.ds(first, count)]
            for way in range(3):
                @pl.when(flags[o][i][way])
                def _():
                    for _ in range(PIECES):
                        pltpu.make_async_copy(part, part, tree_send.at[o, i, way]).wait()

        @pl.when(core == o)
        def _():
            part = ahead.at[o, pl.ds(0, CHIPS - 1)]
            pltpu.make_async_copy(part, part, ahead_send.at[o]).wait()

        @pl.when(core != o)
        def _():
            part = ahead.at[o]
            pltpu.make_async_copy(part, part, ahead_send.at[o]).wait()

    part = back.at[pl.ds(0, 31 * PLANES)]
    pltpu.make_async_copy(part, part, back_send.at[0]).wait()
    for h in range(2):
        pltpu.make_async_copy(
            result.at[pl.ds(h * half, half)], out_ref.at[0, pl.ds(h * half, half)], out_sem.at[h]
        ).wait()


def constants():
    positions = np.arange(POINTS)[:, None] * (np.arange(FREQS) - FREQS // 2)[None, :] % POINTS
    angles = positions * (2.0 * math.pi / POINTS)
    cas = np.cos(angles) + np.sin(angles)
    high = cas.astype(ml_dtypes.bfloat16)
    low = (cas - high.astype(np.float64)).astype(ml_dtypes.bfloat16)
    tall = np.concatenate([high, low], axis=1)
    wide = np.concatenate([high.T, low.T], axis=0)
    return tall, wide


def exchange(number, roots):
    dma = pltpu.SemaphoreType.DMA
    return pl.pallas_call(
        functools.partial(kernel, roots),
        out_shape=jax.ShapeDtypeStruct((1, PLANES, POINTS, POINTS), F32),
        in_specs=[
            pl.BlockSpec(memory_space=pl.ANY),
            pl.BlockSpec(memory_space=pl.ANY),
            pl.BlockSpec(memory_space=pl.ANY),
        ],
        out_specs=pl.BlockSpec(memory_space=pl.ANY),
        scratch_shapes=[
            pltpu.VMEM((POINTS, 2 * FREQS), BF16),
            pltpu.VMEM((2 * FREQS, POINTS), BF16),
            pltpu.VMEM((2, PLANES, POINTS, POINTS), F32),
            pltpu.VMEM((PLANES, POINTS, POINTS), F32),
            pltpu.VMEM((2, CHIPS, PLANES, 8, FREQS), F32),
            pltpu.VMEM((POINTS, 8, FREQS), F32),
            pltpu.VMEM((POINTS, 8, FREQS), F32),
            pltpu.VMEM((2, CHIPS, PLANES, 8, FREQS), F32),
            pltpu.VMEM((8, FREQS, FREQS), F32),
            pltpu.VMEM((PLANES, POINTS, POINTS), F32),
            pltpu.VMEM((PLANES, POINTS, POINTS), F32),
            dma((5,)), dma((2, 3, 3)), dma((2, PLANES * PIECES, 3)),
            dma((2,)), dma((1,)), dma((1,)), dma((2, 2)), dma((2,)),
        ],
        compiler_params=pltpu.CompilerParams(
            collective_id=number, has_side_effects=True, vmem_limit_bytes=VMEM_MIB << 20
        ),
    )


PAIRS = tuple(itertools.combinations(range(8), 2))


def per_device(orbitals, band_ids, owners):
    tall, wide = (jnp.asarray(c) for c in constants())
    is_owner = jnp.any(band_ids[:, None] == owners[None, :], axis=1)
    slots = jnp.arange(8, dtype=jnp.int32)
    low = jnp.min(jnp.where(is_owner, slots, 8))
    high = jnp.max(jnp.where(is_owner, slots, -1))
    which = low * (15 - low) // 2 + high - low - 1
    branches = [exchange(n, pair) for n, pair in enumerate(PAIRS)]
    return lax.switch(which, branches, orbitals, tall, wide)


def solution(mesh):
    placed = (P("band", "fft", None, None), P(), P())
    return jax.shard_map(
        per_device,
        mesh=mesh,
        in_specs=placed,
        out_specs=P("band", "fft", None, None),
        check_vma=False,
    )
```

```python
import math

import jax
import jax.numpy as jnp
import ml_dtypes
import numpy as np
from jax import lax
from jax.experimental import pallas as pl
from jax.experimental.pallas import tpu as pltpu
from jax.sharding import PartitionSpec as P

MESH = pl.DeviceIdType.MESH
F32 = jnp.float32
BF16 = jnp.bfloat16
cell_length = 46.9

POINTS = 256
FREQS = 128
PLANES = 8
CHIPS = 16
VMEM_MIB = 60
ROWS = ((0, 88), (88, 88), (176, 80))
ORDER = (0, 1, 2, 5, 6, 3, 4, 7)
EARLY = 5
TREES = (
    ((0, 2, 4, 5), (3,), (2, 4)),
    ((7,), (0, 6, 4, 7, 5), (6,)),
    ((1, 3), (1,), (0, 3, 5, 7)),
)
DEPTHS = ((0, 3, 1, 2, 2, 3, 3, 4), (0, 3, 3, 4, 2, 3, 1, 2), (0, 1, 3, 2, 4, 3, 3, 2))


def split(value):
    high = value.astype(BF16)
    return high, (value - high.astype(F32)).astype(BF16)


def dot(left, right):
    return jnp.dot(left, right, preferred_element_type=F32)


def quarters(value):
    rows, columns = value.shape[0] // 2, value.shape[1] // 2
    small = (value[:rows, columns:] + value[rows:, :columns]) + value[rows:, columns:]
    return value[:rows, :columns] + small


def kernel(
    orb_ref, ids_ref, owners_ref, tall_in, wide_in, tall_x_in, wide_x_in, out_ref,
    tall_ref, wide_ref, tall_x, wide_x, gathered, held, own, ahead, arrived, back, restored, weights, partial, result,
    in_sem, spread_send, spread_recv, tree_send, tree_recv, ahead_send, ahead_recv, back_send, back_recv, out_sem,
):
    band = lax.axis_index("band")
    place = lax.axis_index("fft")
    my_x, my_y = band // 2, band % 2
    chip, core = place // 2, place % 2

    def band_at(x, y):
        return ((my_x + x) % 4) * 2 + (my_y + y) % 2

    def source(relative):
        return band_at(4 - relative // 2, relative % 2)

    neighbours = (band_at(1, 0), band_at(3, 0), band_at(0, 1))

    load = pltpu.make_async_copy(orb_ref.at[0], own, in_sem.at[0])
    load.start()
    tables = (
        pltpu.make_async_copy(tall_in, tall_ref, in_sem.at[1]),
        pltpu.make_async_copy(wide_in, wide_ref, in_sem.at[2]),
        pltpu.make_async_copy(tall_x_in.at[band], tall_x, in_sem.at[3]),
        pltpu.make_async_copy(wide_x_in.at[band], wide_x, in_sem.at[4]),
    )
    for table in tables:
        table.start()
    barrier = pltpu.get_barrier_semaphore()
    for k in range(1, 8):
        pl.semaphore_signal(
            barrier, inc=1, device_id=((band + k) % 8, place), device_id_type=MESH
        )

    def greet(k, _):
        pl.semaphore_signal(
            barrier, inc=1, device_id=(band, (place + k) % 32), device_id_type=MESH
        )
        return 0

    lax.fori_loop(1, 32, greet, 0)

    pl.semaphore_wait(barrier, 38)
    for relative in (4, 5, 2, 6, 3, 7, 1):
        there = source(relative)
        pltpu.make_async_remote_copy(
            src_ref=orb_ref.at[0, there], dst_ref=gathered.at[band],
            send_sem=spread_send.at[0], recv_sem=spread_recv.at[0],
            device_id=(there, place), device_id_type=MESH,
        ).start()

    kx = lax.broadcasted_iota(jnp.int32, (FREQS, FREQS), 0) - FREQS // 2
    kz = lax.broadcasted_iota(jnp.int32, (FREQS, FREQS), 1) - FREQS // 2

    def weigh(row, _):
        ky = chip * 8 + row - FREQS // 2
        square = kx * kx + kz * kz + ky * ky
        inside = (square > 0) & (square < FREQS * FREQS // 4)
        safe = jnp.where(inside, square, 1).astype(F32)
        scale = cell_length**2 / math.pi / float(POINTS) ** 3
        weights[row] = jnp.where(inside, jnp.float32(scale) / safe, jnp.float32(0.0))
        return 0

    lax.fori_loop(0, 8, weigh, 0)

    load.wait()
    for table in tables:
        table.wait()
    gathered[band] = own[band]
    part = gathered.at[pl.ds(0, 7)]
    pltpu.make_async_copy(part, part, spread_recv.at[0]).wait()
    for o in range(2):
        slot = 0
        for s in range(1, 8):
            slot = jnp.where(ids_ref[s] == owners_ref[o], s, slot)
        held[o, band] = gathered[slot]

    def relay(o, depth):
        for i, (first, count) in enumerate(ROWS):
            for relative in range(8):
                if DEPTHS[i][relative] != depth:
                    continue
                origin = source(relative)
                part = held.at[o, origin, pl.ds(first, count)]
                if depth:
                    pltpu.make_async_copy(part, part, tree_recv.at[o, origin, i]).wait()
                for way in range(3):
                    if relative in TREES[i][way]:
                        pltpu.make_async_remote_copy(
                            src_ref=part, dst_ref=part,
                            send_sem=tree_send.at[o], recv_sem=tree_recv.at[o, origin, i],
                            device_id=(neighbours[way], place), device_id_type=MESH,
                        ).start()

    def plane(k):
        return source(sum(jnp.where(k == n, relative, 0) for n, relative in enumerate(ORDER)))

    def forward(o, k):
        p = plane(k)
        density = held[o, p] * own[p]
        level = jnp.sum(density, keepdims=True) * (1.0 / POINTS**2)
        high, low = split(density - level)
        along_z = quarters(dot(jnp.concatenate([high, low], axis=0), tall_ref[...]))
        high, low = split(along_z)
        along_y = quarters(dot(wide_ref[...], jnp.concatenate([high, low], axis=1)))
        along_y = along_y + jnp.where((kx == 0) & (kz == 0), level * float(POINTS**2), 0.0)
        ahead[o, :, k] = along_y.reshape(CHIPS, 8, FREQS)

    def send_ahead(o, first, count):
        def one(k, _):
            there = (chip + k) % CHIPS
            source = ahead.at[o, there, pl.ds(first, count)]
            target = arrived.at[pl.ds(place * PLANES + first, count)]
            here = there * 2 + o == place

            @pl.when(here)
            def _():
                pltpu.make_async_copy(source, target, ahead_recv.at[0]).start()

            @pl.when(jnp.logical_not(here))
            def _():
                pltpu.make_async_remote_copy(
                    src_ref=source, dst_ref=target,
                    send_sem=ahead_send.at[o], recv_sem=ahead_recv.at[0],
                    device_id=(band, there * 2 + o), device_id_type=MESH,
                ).start()

            return 0

        lax.fori_loop(0, CHIPS, one, 0)

    def transform(o, first, last):
        def one(k, _):
            forward(o, k)
            return 0

        lax.fori_loop(first, last, one, 0)
        send_ahead(o, first, last - first)

    half = PLANES // 2

    def middle(o):
        @pl.when(core == o)
        def _():
            pltpu.make_async_copy(arrived, arrived, ahead_recv.at[0]).wait()

            def one(row, _):
                column = arrived[:, pl.ds(row, 1), :].reshape(POINTS, FREQS)
                level = jnp.sum(column, axis=0, keepdims=True) * (1.0 / POINTS)
                high, low = split(column - level)
                along_x = quarters(dot(wide_x[...], jnp.concatenate([high, low], axis=1)))
                along_x = along_x + jnp.where(kx == 0, level * float(POINTS), 0.0)
                high, low = split(along_x * weights[row])
                pair = jnp.concatenate([high, low], axis=1)
                both = dot(tall_x[...], jnp.concatenate([pair, pair], axis=0))
                back[:, pl.ds(row, 1), :] = (both[:, :FREQS] + both[:, FREQS:]).reshape(POINTS, 1, FREQS)
                return 0

            lax.fori_loop(0, 8, one, 0, unroll=True)
            for h in range(2):
                def one(k, _):
                    there = (place + k) % 32
                    source = back.at[pl.ds(there * PLANES + h * half, half)]
                    target = restored.at[o, chip, pl.ds(h * half, half)]

                    @pl.when(k == 0)
                    def _():
                        pltpu.make_async_copy(source, target, back_recv.at[o, h]).start()

                    @pl.when(k != 0)
                    def _():
                        pltpu.make_async_remote_copy(
                            src_ref=source, dst_ref=target,
                            send_sem=back_send.at[0], recv_sem=back_recv.at[o, h],
                            device_id=(band, there), device_id_type=MESH,
                        ).start()

                    return 0

                lax.fori_loop(0, 32, one, 0)

    def backward(o, k):
        high, low = split(restored[o, :, k].reshape(FREQS, FREQS))
        pair = jnp.concatenate([high, low], axis=1)
        both = dot(tall_ref[...], jnp.concatenate([pair, pair], axis=0))
        high, low = split(both[:, :FREQS] + both[:, FREQS:])
        field = dot(jnp.concatenate([high, low], axis=1), jnp.concatenate([wide_ref[:FREQS], wide_ref[:FREQS]], axis=0))
        field = field + dot(high, wide_ref[FREQS:])
        return held[o, plane(k)] * field
        return held[o, plane(k)]

    relay(0, 0)
    relay(1, 0)
    relay(0, 1)
    relay(0, 2)
    relay(1, 1)
    relay(0, 3)
    transform(0, 0, EARLY)
    relay(1, 2)
    relay(0, 4)
    transform(0, EARLY, PLANES)
    relay(1, 3)
    transform(1, 0, EARLY)
    relay(1, 4)
    transform(1, EARLY, PLANES)
    middle(0)
    middle(1)

    for h in range(2):
        part = restored.at[0, :, pl.ds(h * half, half)]
        pltpu.make_async_copy(part, part, back_recv.at[0, h]).wait()

        def one(k, _):
            partial[k] = backward(0, k)
            return 0

        lax.fori_loop(h * half, (h + 1) * half, one, 0)
    for h in range(2):
        part = restored.at[1, :, pl.ds(h * half, half)]
        pltpu.make_async_copy(part, part, back_recv.at[1, h]).wait()

        def one(k, _):
            p = plane(k)
            result[p] = -(partial[k] + backward(1, k))
            pltpu.make_async_copy(result.at[p], out_ref.at[0, p], out_sem.at[0]).start()
            return 0

        lax.fori_loop(h * half, (h + 1) * half, one, 0)

    part = gathered.at[pl.ds(0, 7)]
    pltpu.make_async_copy(part, part, spread_send.at[0]).wait()
    for o in range(2):
        part = held.at[o, pl.ds(0, 7)]
        pltpu.make_async_copy(part, part, tree_send.at[o]).wait()

        @pl.when(core == o)
        def _():
            part = ahead.at[o, pl.ds(0, CHIPS - 1)]
            pltpu.make_async_copy(part, part, ahead_send.at[o]).wait()

        @pl.when(core != o)
        def _():
            part = ahead.at[o]
            pltpu.make_async_copy(part, part, ahead_send.at[o]).wait()

    part = back.at[pl.ds(0, 31 * PLANES)]
    pltpu.make_async_copy(part, part, back_send.at[0]).wait()
    pltpu.make_async_copy(result, out_ref.at[0], out_sem.at[0]).wait()


def constants():
    positions = np.arange(POINTS)[:, None] * (np.arange(FREQS) - FREQS // 2)[None, :] % POINTS
    angles = positions * (2.0 * math.pi / POINTS)
    cas = np.cos(angles) + np.sin(angles)
    high = cas.astype(ml_dtypes.bfloat16)
    low = (cas - high.astype(np.float64)).astype(ml_dtypes.bfloat16)
    tall = np.concatenate([high, low], axis=1)
    wide = np.concatenate([high.T, low.T], axis=0)
    tall_x, wide_x = [], []
    for band in range(8):
        planes = [((band // 2 - r // 2) % 4) * 2 + (band + r) % 2 for r in ORDER]
        rows = np.concatenate([block * PLANES + np.array(planes) for block in range(POINTS // PLANES)])
        tall_x.append(tall[rows])
        wide_x.append(wide[:, rows])
    return tall, wide, np.stack(tall_x), np.stack(wide_x)


def exchange():
    dma = pltpu.SemaphoreType.DMA
    return pl.pallas_call(
        kernel,
        out_shape=jax.ShapeDtypeStruct((1, PLANES, POINTS, POINTS), F32),
        in_specs=[
            pl.BlockSpec(memory_space=pl.ANY),
            pl.BlockSpec(memory_space=pltpu.SMEM),
            pl.BlockSpec(memory_space=pltpu.SMEM),
            pl.BlockSpec(memory_space=pl.ANY),
            pl.BlockSpec(memory_space=pl.ANY),
            pl.BlockSpec(memory_space=pl.ANY),
            pl.BlockSpec(memory_space=pl.ANY),
        ],
        out_specs=pl.BlockSpec(memory_space=pl.ANY),
        scratch_shapes=[
            pltpu.VMEM((POINTS, 2 * FREQS), BF16),
            pltpu.VMEM((2 * FREQS, POINTS), BF16),
            pltpu.VMEM((POINTS, 2 * FREQS), BF16),
            pltpu.VMEM((2 * FREQS, POINTS), BF16),
            pltpu.VMEM((8, POINTS, POINTS), F32),
            pltpu.VMEM((2, PLANES, POINTS, POINTS), F32),
            pltpu.VMEM((PLANES, POINTS, POINTS), F32),
            pltpu.VMEM((2, CHIPS, PLANES, 8, FREQS), F32),
            pltpu.VMEM((POINTS, 8, FREQS), F32),
            pltpu.VMEM((POINTS, 8, FREQS), F32),
            pltpu.VMEM((2, CHIPS, PLANES, 8, FREQS), F32),
            pltpu.VMEM((8, FREQS, FREQS), F32),
            pltpu.VMEM((PLANES, POINTS, POINTS), F32),
            pltpu.VMEM((PLANES, POINTS, POINTS), F32),
            dma((5,)), dma((1,)), dma((1,)), dma((2,)), dma((2, 8, 3)),
            dma((2,)), dma((1,)), dma((1,)), dma((2, 2)), dma((1,)),
        ],
        compiler_params=pltpu.CompilerParams(
            collective_id=0, has_side_effects=True, vmem_limit_bytes=VMEM_MIB << 20
        ),
    )


def per_device(orbitals, band_ids, owners):
    tables = [jnp.asarray(c) for c in constants()]
    return exchange()(orbitals, band_ids, owners, *tables)


def solution(mesh):
    placed = (P("band", "fft", None, None), P(), P())
    return jax.shard_map(
        per_device,
        mesh=mesh,
        in_specs=placed,
        out_specs=P("band", "fft", None, None),
        check_vma=False,
    )
```

```python
import itertools
import math

import jax
import jax.numpy as jnp
import ml_dtypes
import numpy as np
from jax import lax
from jax.experimental import pallas as pl
from jax.experimental.pallas import tpu as pltpu
from jax.sharding import PartitionSpec as P

MESH = pl.DeviceIdType.MESH
F32 = jnp.float32
BF16 = jnp.bfloat16
cell_length = 46.9

POINTS = 256
FREQS = 128
PLANES = 8
CHIPS = 16
VMEM_MIB = 60
T_ROWS = ((0, 88), (88, 88), (176, 80))
T_TREES = (
    ((0, 2, 4, 5), (3,), (2, 4)),
    ((7,), (0, 6, 4, 7, 5), (6,)),
    ((1, 3), (1,), (0, 3, 5, 7)),
)
T_DEPTHS = ((0, 3, 1, 2, 2, 3, 3, 4), (0, 3, 3, 4, 2, 3, 1, 2), (0, 1, 3, 2, 4, 3, 3, 2))
T_ORDER = (0, 1, 2, 5, 6, 3, 4, 7)
U_ROWS = ((0, 128), (128, 128))
U_TREES = (((0, 2, 1, 3), (0, 1), (0,)), ((0, 1), (0, 6, 1, 7), (0,)))
U_DEPTHS = ((0, 1, 1, 2, 2, 3, 1, 2), (0, 1, 1, 2, 2, 3, 1, 2))
U_ORDER = (0, 1, 2, 6, 3, 7, 4, 5)
T, U = (T_ROWS, T_TREES, T_DEPTHS, T_ORDER), (U_ROWS, U_TREES, U_DEPTHS, U_ORDER)
SCHEMES = (T, T)
PROGRAM = (
    ("r", 0, 0), ("r", 1, 0), ("r", 0, 1), ("r", 0, 2), ("r", 1, 1), ("r", 0, 3), ("t", 0, 0, 5), ("r", 1, 2),
    ("r", 0, 4), ("t", 0, 5, 8), ("r", 1, 3), ("t", 1, 0, 5), ("r", 1, 4), ("t", 1, 5, 8), ("m", 0), ("m", 1),
)


SENT = 7


def ky_of(block, row):
    plain = 6 * block + row - 48
    plain = jnp.where(plain == -48, -64, plain)
    inner = jnp.where(block < 8, 48 + block, -40 - block)
    outer = jnp.where(block < 8, 63 - block, block - 71)
    return jnp.where(row < 6, plain, jnp.where(row == 6, inner, outer))


def split(value):
    high = value.astype(BF16)
    return high, (value - high.astype(F32)).astype(BF16)


def dot(left, right):
    return jnp.dot(left, right, preferred_element_type=F32)


def quarters(value):
    rows, columns = value.shape[0] // 2, value.shape[1] // 2
    small = (value[:rows, columns:] + value[rows:, :columns]) + value[rows:, columns:]
    return value[:rows, :columns] + small


def kernel(
    orb_ref, ids_ref, owners_ref, tall_in, wide_in, tall_y_in, wide_y_in, tall_x_in, wide_x_in, out_ref,
    tall_ref, wide_ref, tall_y, wide_y, tall_x, wide_x, gathered, held, own, ahead, arrived, back, restored, weights, partial,
    in_sem, met, spread_send, spread_recv, tree_send, tree_recv, ahead_send, ahead_recv, back_send, back_recv,
):
    band = lax.axis_index("band")
    place = lax.axis_index("fft")
    my_x, my_y = band // 2, band % 2
    chip, core = place // 2, place % 2

    def band_at(x, y):
        return ((my_x + x) % 4) * 2 + (my_y + y) % 2

    def source(relative):
        return band_at(4 - relative // 2, relative % 2)

    def flipped(bit):
        step = 1 << bit
        return place + step - 2 * step * ((place // step) % 2)

    neighbours = (band_at(1, 0), band_at(3, 0), band_at(0, 1))

    load = pltpu.make_async_copy(orb_ref.at[0], own, in_sem.at[0])
    load.start()
    tables = (
        pltpu.make_async_copy(tall_in, tall_ref, in_sem.at[1]),
        pltpu.make_async_copy(wide_in, wide_ref, in_sem.at[2]),
        pltpu.make_async_copy(tall_y_in, tall_y, in_sem.at[5]),
        pltpu.make_async_copy(wide_y_in, wide_y, in_sem.at[6]),
        pltpu.make_async_copy(tall_x_in.at[core, band], tall_x, in_sem.at[3]),
        pltpu.make_async_copy(wide_x_in.at[core, band], wide_x, in_sem.at[4]),
    )
    for table in tables:
        table.start()
    barrier = pltpu.get_barrier_semaphore()
    for k in range(1, 8):
        pl.semaphore_signal(
            barrier, inc=1, device_id=((band + k) % 8, place), device_id_type=MESH
        )

    for bit in range(5):
        pl.semaphore_signal(
            barrier, inc=1, device_id=(band, flipped(bit)), device_id_type=MESH
        )
    pl.semaphore_wait(barrier, 12)
    for relative in (4, 5, 2, 6, 3, 7, 1):
        there = source(relative)
        pltpu.make_async_remote_copy(
            src_ref=orb_ref.at[0, there], dst_ref=gathered.at[band],
            send_sem=spread_send.at[0], recv_sem=spread_recv.at[0],
            device_id=(there, place), device_id_type=MESH,
        ).start()

    kx = lax.broadcasted_iota(jnp.int32, (FREQS, FREQS), 0) - FREQS // 2
    kz = lax.broadcasted_iota(jnp.int32, (FREQS, FREQS), 1) - FREQS // 2

    turned = (kz + FREQS) % FREQS - FREQS // 2

    def weigh(row, _):
        ky, ky_outer = ky_of(chip, row), ky_of(chip, 7)
        outside = (row == 6) & (ky * ky + kz * kz >= FREQS * FREQS // 4)
        square = jnp.where(
            outside, ky_outer * ky_outer + turned * turned, ky * ky + kz * kz
        ) + kx * kx
        inside = (square > 0) & (square < FREQS * FREQS // 4)
        safe = jnp.where(inside, square, 1).astype(F32)
        scale = cell_length**2 / math.pi / float(POINTS) ** 3
        weights[row] = jnp.where(inside, jnp.float32(scale) / safe, jnp.float32(0.0))
        return 0

    row_in = (kx + FREQS // 2) % 8
    ky = ky_of((kx + FREQS // 2) // 8, row_in)
    in_disc = ky * ky + kz * kz < FREQS * FREQS // 4
    take_outer = (row_in == 6) & jnp.logical_not(in_disc)

    lax.fori_loop(0, SENT, weigh, 0)

    for bit in range(5):
        pl.semaphore_signal(
            met.at[bit], inc=1, device_id=(band, flipped(bit)), device_id_type=MESH
        )
        pl.semaphore_wait(met.at[bit], 1)

    load.wait()
    for table in tables:
        table.wait()
    gathered[band] = own[band]
    part = gathered.at[pl.ds(0, 7)]
    pltpu.make_async_copy(part, part, spread_recv.at[0]).wait()
    for o in range(2):
        slot = 0
        for s in range(1, 8):
            slot = jnp.where(ids_ref[s] == owners_ref[o], s, slot)
        held[o, band] = gathered[slot]

    def relay(o, depth):
        table, trees, depths, _ = SCHEMES[o]
        for i, (first, count) in enumerate(table):
            for relative in range(8):
                if depths[i][relative] != depth:
                    continue
                origin = source(relative)
                part = held.at[o, origin, pl.ds(first, count)]
                if depth:
                    pltpu.make_async_copy(part, part, tree_recv.at[o, origin, i]).wait()
                for way in range(3):
                    if relative in trees[i][way]:
                        pltpu.make_async_remote_copy(
                            src_ref=part, dst_ref=part,
                            send_sem=tree_send.at[o], recv_sem=tree_recv.at[o, origin, i],
                            device_id=(neighbours[way], place), device_id_type=MESH,
                        ).start()

    def plane(o, k):
        return source(sum(jnp.where(k == n, relative, 0) for n, relative in enumerate(SCHEMES[o][3])))

    def forward(o, k):
        p = plane(o, k)
        density = held[o, p] * own[p]
        level = jnp.sum(density, keepdims=True) * (1.0 / POINTS**2)
        high, low = split(density - level)
        along_z = quarters(dot(jnp.concatenate([high, low], axis=0), tall_ref[...]))
        high, low = split(along_z)
        along_y = quarters(dot(wide_y[...], jnp.concatenate([high, low], axis=1)))
        along_y = along_y + jnp.where((kx == 0) & (kz == 0), level * float(POINTS**2), 0.0)
        outer = pltpu.roll(pltpu.roll(along_y, FREQS - 1, 0), FREQS // 2, 1)
        along_y = jnp.where(take_outer, outer, along_y)
        ahead[o, :, k] = along_y.reshape(CHIPS, 8, FREQS)

    def send_ahead(o, first, count):
        def one(k, _):
            there = (chip + k) % CHIPS
            source = ahead.at[o, there, pl.ds(first, count), pl.ds(0, SENT)]
            target = arrived.at[pl.ds(place * PLANES + first, count), pl.ds(0, SENT)]
            here = there * 2 + o == place

            @pl.when(here)
            def _():
                pltpu.make_async_copy(source, target, ahead_recv.at[0]).start()

            @pl.when(jnp.logical_not(here))
            def _():
                pltpu.make_async_remote_copy(
                    src_ref=source, dst_ref=target,
                    send_sem=ahead_send.at[o], recv_sem=ahead_recv.at[0],
                    device_id=(band, there * 2 + o), device_id_type=MESH,
                ).start()

            return 0

        lax.fori_loop(0, CHIPS, one, 0)

    def transform(o, first, last):
        def one(k, _):
            forward(o, k)
            return 0

        lax.fori_loop(first, last, one, 0)
        send_ahead(o, first, last - first)

    half = PLANES // 2

    def middle(o):
        @pl.when(core == o)
        def _():
            landed = arrived.at[:, pl.ds(0, SENT)]
            pltpu.make_async_copy(landed, landed, ahead_recv.at[0]).wait()

            def one(row, _):
                column = arrived[:, pl.ds(row, 1), :].reshape(POINTS, FREQS)
                level = jnp.sum(column, axis=0, keepdims=True) * (1.0 / POINTS)
                high, low = split(column - level)
                along_x = quarters(dot(wide_x[...], jnp.concatenate([high, low], axis=1)))
                along_x = along_x + jnp.where(kx == 0, level * float(POINTS), 0.0)
                high, low = split(along_x * weights[row])
                pair = jnp.concatenate([high, low], axis=1)
                both = dot(tall_x[...], jnp.concatenate([pair, pair], axis=0))
                back[:, pl.ds(row, 1), :] = (both[:, :FREQS] + both[:, FREQS:]).reshape(POINTS, 1, FREQS)
                return 0

            lax.fori_loop(0, SENT, one, 0, unroll=True)
            for h in range(2):
                def one(k, _):
                    there = (place + k) % 32
                    source = back.at[pl.ds(there * PLANES + h * half, half), pl.ds(0, SENT)]
                    target = restored.at[o, chip, pl.ds(h * half, half), pl.ds(0, SENT)]

                    @pl.when(k == 0)
                    def _():
                        pltpu.make_async_copy(source, target, back_recv.at[o, h]).start()

                    @pl.when(k != 0)
                    def _():
                        pltpu.make_async_remote_copy(
                            src_ref=source, dst_ref=target,
                            send_sem=back_send.at[0], recv_sem=back_recv.at[o, h],
                            device_id=(band, there), device_id_type=MESH,
                        ).start()

                    return 0

                lax.fori_loop(0, 32, one, 0)

    def backward(o, k):
        coeffs = restored[o, :, k].reshape(FREQS, FREQS)
        outer = pltpu.roll(pltpu.roll(coeffs, 1, 0), FREQS // 2, 1)
        coeffs = jnp.where(in_disc, jnp.where(row_in == 7, outer, coeffs), 0.0)
        high, low = split(coeffs)
        pair = jnp.concatenate([high, low], axis=1)
        both = dot(tall_y[...], jnp.concatenate([pair, pair], axis=0))
        high, low = split(both[:, :FREQS] + both[:, FREQS:])
        field = dot(jnp.concatenate([high, low], axis=1), jnp.concatenate([wide_ref[:FREQS], wide_ref[:FREQS]], axis=0))
        field = field + dot(high, wide_ref[FREQS:])
        return held[o, plane(o, k)] * field

    for name, *numbers in PROGRAM:
        {"r": relay, "t": transform, "m": middle}[name](*numbers)

    for h in range(2):
        part = restored.at[0, :, pl.ds(h * half, half), pl.ds(0, SENT)]
        pltpu.make_async_copy(part, part, back_recv.at[0, h]).wait()

        def one(k, _):
            partial[plane(0, k)] = backward(0, k)
            return 0

        lax.fori_loop(h * half, (h + 1) * half, one, 0)
    for h in range(2):
        part = restored.at[1, :, pl.ds(h * half, half), pl.ds(0, SENT)]
        pltpu.make_async_copy(part, part, back_recv.at[1, h]).wait()

        def one(k, _):
            p = plane(1, k)
            out_ref[0, p] = -(partial[p] + backward(1, k))
            return 0

        lax.fori_loop(h * half, (h + 1) * half, one, 0)

    part = gathered.at[pl.ds(0, 7)]
    pltpu.make_async_copy(part, part, spread_send.at[0]).wait()
    for o in range(2):
        part = held.at[o, pl.ds(0, 7)]
        pltpu.make_async_copy(part, part, tree_send.at[o]).wait()

        @pl.when(core == o)
        def _():
            part = ahead.at[o, pl.ds(0, CHIPS - 1), :, pl.ds(0, SENT)]
            pltpu.make_async_copy(part, part, ahead_send.at[o]).wait()

        @pl.when(core != o)
        def _():
            part = ahead.at[o, :, :, pl.ds(0, SENT)]
            pltpu.make_async_copy(part, part, ahead_send.at[o]).wait()

    part = back.at[pl.ds(0, 31 * PLANES), pl.ds(0, SENT)]
    pltpu.make_async_copy(part, part, back_send.at[0]).wait()


def cas_tables(freqs):
    positions = np.arange(POINTS)[:, None] * freqs[None, :] % POINTS
    angles = positions * (2.0 * math.pi / POINTS)
    cas = np.cos(angles) + np.sin(angles)
    high = cas.astype(ml_dtypes.bfloat16)
    low = (cas - high.astype(np.float64)).astype(ml_dtypes.bfloat16)
    tall = np.concatenate([high, low], axis=1)
    wide = np.concatenate([high.T, low.T], axis=0)
    return tall, wide


def constants():
    tall, wide = cas_tables(np.arange(FREQS) - FREQS // 2)
    ky = []
    for block in range(CHIPS):
        ky += [6 * block + row - 48 for row in range(6)]
        ky += [48 + block, 63 - block] if block < 8 else [-40 - block, block - 71]
    ky[0] = -64
    tall_y, wide_y = cas_tables(np.array(ky))
    tall_x, wide_x = [], []
    for o, band in itertools.product(range(2), range(8)):
        planes = [((band // 2 - r // 2) % 4) * 2 + (band + r) % 2 for r in SCHEMES[o][3]]
        rows = np.concatenate([block * PLANES + np.array(planes) for block in range(POINTS // PLANES)])
        tall_x.append(tall[rows])
        wide_x.append(wide[:, rows])
    return tall, wide, tall_y, wide_y, np.reshape(tall_x, (2, 8, *tall.shape)), np.reshape(wide_x, (2, 8, *wide.shape))


def exchange():
    dma = pltpu.SemaphoreType.DMA
    return pl.pallas_call(
        kernel,
        out_shape=jax.ShapeDtypeStruct((1, PLANES, POINTS, POINTS), F32),
        in_specs=[
            pl.BlockSpec(memory_space=pl.ANY),
            pl.BlockSpec(memory_space=pltpu.SMEM),
            pl.BlockSpec(memory_space=pltpu.SMEM),
            pl.BlockSpec(memory_space=pl.ANY),
            pl.BlockSpec(memory_space=pl.ANY),
            pl.BlockSpec(memory_space=pl.ANY),
            pl.BlockSpec(memory_space=pl.ANY),
            pl.BlockSpec(memory_space=pl.ANY),
            pl.BlockSpec(memory_space=pl.ANY),
        ],
        out_specs=pl.BlockSpec(memory_space=pltpu.VMEM),
        scratch_shapes=[
            pltpu.VMEM((POINTS, 2 * FREQS), BF16),
            pltpu.VMEM((2 * FREQS, POINTS), BF16),
            pltpu.VMEM((POINTS, 2 * FREQS), BF16),
            pltpu.VMEM((2 * FREQS, POINTS), BF16),
            pltpu.VMEM((POINTS, 2 * FREQS), BF16),
            pltpu.VMEM((2 * FREQS, POINTS), BF16),
            pltpu.VMEM((8, POINTS, POINTS), F32),
            pltpu.VMEM((2, PLANES, POINTS, POINTS), F32),
            pltpu.VMEM((PLANES, POINTS, POINTS), F32),
            pltpu.VMEM((2, CHIPS, PLANES, 8, FREQS), F32),
            pltpu.VMEM((POINTS, 8, FREQS), F32),
            pltpu.VMEM((POINTS, 8, FREQS), F32),
            pltpu.VMEM((2, CHIPS, PLANES, 8, FREQS), F32),
            pltpu.VMEM((8, FREQS, FREQS), F32),
            pltpu.VMEM((PLANES, POINTS, POINTS), F32),
            dma((7,)), pltpu.SemaphoreType.REGULAR((5,)), dma((1,)), dma((1,)), dma((2,)), dma((2, 8, 3)),
            dma((2,)), dma((1,)), dma((1,)), dma((2, 2)),
        ],
        compiler_params=pltpu.CompilerParams(
            collective_id=0, has_side_effects=True, vmem_limit_bytes=VMEM_MIB << 20
        ),
    )


def per_device(orbitals, band_ids, owners):
    tables = [jnp.asarray(c) for c in constants()]
    return exchange()(orbitals, band_ids, owners, *tables)


def solution(mesh):
    placed = (P("band", "fft", None, None), P(), P())
    return jax.shard_map(
        per_device,
        mesh=mesh,
        in_specs=placed,
        out_specs=P("band", "fft", None, None),
        check_vma=False,
    )
```

```python
import itertools
import math

import jax
import jax.numpy as jnp
import ml_dtypes
import numpy as np
from jax import lax
from jax.experimental import pallas as pl
from jax.experimental.pallas import tpu as pltpu
from jax.sharding import PartitionSpec as P

MESH = pl.DeviceIdType.MESH
F32 = jnp.float32
BF16 = jnp.bfloat16
cell_length = 46.9

POINTS = 256
FREQS = 128
PLANES = 8
CHIPS = 16
VMEM_MIB = 50
T_TREES = (
    ((0, 2, 4, 5), (3,), (2, 4)),
    ((7,), (0, 6, 4, 7, 5), (6,)),
    ((1, 3), (1,), (0, 3, 5, 7)),
)
T_DEPTHS = ((0, 3, 1, 2, 2, 3, 3, 4), (0, 3, 3, 4, 2, 3, 1, 2), (0, 1, 3, 2, 4, 3, 3, 2))
T_ORDER = (0, 1, 2, 5, 6, 3, 4, 7)
W = (((0, 48), (48, 40), (88, 40), (128, 40), (168, 48), (216, 40)), T_TREES * 2, T_DEPTHS * 2, T_ORDER)
SCHEMES = (W, W)
PROGRAM = (
    ("r", 0, 0), ("r", 1, 0), ("r", 0, 1), ("r", 0, 2), ("r", 1, 1), ("r", 0, 3), ("t", 0, 0, 5), ("r", 1, 2),
    ("r", 0, 4), ("t", 0, 5, 8), ("r", 1, 3), ("t", 1, 0, 5), ("r", 1, 4), ("t", 1, 5, 8), ("m", 0),
    ("b", 0, 0), ("b", 0, 1), ("m", 1), ("b", 1, 0), ("b", 1, 1), ("b", 1, 2), ("b", 1, 3),
)


SENT = 7
UNROLL = True
RETURNS = (2, 4)


def ky_of(block, row):
    plain = 6 * block + row - 48
    plain = jnp.where(plain == -48, -64, plain)
    inner = jnp.where(block < 8, 48 + block, -40 - block)
    outer = jnp.where(block < 8, 63 - block, block - 71)
    return jnp.where(row < 6, plain, jnp.where(row == 6, inner, outer))


def split(value):
    high = value.astype(BF16)
    return high, (value - high.astype(F32)).astype(BF16)


def dot(left, right):
    return jnp.dot(left, right, preferred_element_type=F32)


def quarters(value):
    rows, columns = value.shape[0] // 2, value.shape[1] // 2
    small = (value[:rows, columns:] + value[rows:, :columns]) + value[rows:, columns:]
    return value[:rows, :columns] + small


def kernel(
    orb_ref, info_in, tables_in, out_ref,
    tall_ref, wide_ref, tall_y, wide_y, tall_x, wide_x, gathered, held, own, ahead, arrived, back, restored, weights, partial,
    info_ref, in_sem, met, spread_send, spread_recv, tree_send, tree_recv, ahead_send, ahead_recv, back_send, back_recv,
):
    band = lax.axis_index("band")
    place = lax.axis_index("fft")
    my_x, my_y = band // 2, band % 2
    chip, core = place // 2, place % 2

    def band_at(x, y):
        return ((my_x + x) % 4) * 2 + (my_y + y) % 2

    def source(relative):
        return band_at(4 - relative // 2, relative % 2)

    def flipped(bit):
        step = 1 << bit
        return place + step - 2 * step * ((place // step) % 2)

    neighbours = (band_at(1, 0), band_at(3, 0), band_at(0, 1))

    load = pltpu.make_async_copy(orb_ref.at[0], own, in_sem.at[0])
    load.start()
    tables = (
        pltpu.make_async_copy(info_in, info_ref, in_sem.at[7]),
        pltpu.make_async_copy(tables_in.at[32], tall_ref, in_sem.at[1]),
        pltpu.make_async_copy(tables_in.at[33], wide_ref, in_sem.at[2]),
        pltpu.make_async_copy(tables_in.at[34], tall_y, in_sem.at[5]),
        pltpu.make_async_copy(tables_in.at[35], wide_y, in_sem.at[6]),
        pltpu.make_async_copy(tables_in.at[core * 8 + band], tall_x, in_sem.at[3]),
        pltpu.make_async_copy(tables_in.at[core * 8 + band + 16], wide_x, in_sem.at[4]),
    )
    for table in tables:
        table.start()
    barrier = pltpu.get_barrier_semaphore()
    for k in range(1, 8):
        pl.semaphore_signal(
            barrier, inc=1, device_id=((band + k) % 8, place), device_id_type=MESH
        )

    for bit in range(5):
        pl.semaphore_signal(
            barrier, inc=1, device_id=(band, flipped(bit)), device_id_type=MESH
        )
    pl.semaphore_wait(barrier, 12)
    for relative in (4, 5, 2, 6, 3, 7, 1):
        there = source(relative)
        pltpu.make_async_remote_copy(
            src_ref=orb_ref.at[0, there], dst_ref=gathered.at[band],
            send_sem=spread_send.at[0], recv_sem=spread_recv.at[0],
            device_id=(there, place), device_id_type=MESH,
        ).start()

    kx = lax.broadcasted_iota(jnp.int32, (FREQS, FREQS), 0) - FREQS // 2
    kz = lax.broadcasted_iota(jnp.int32, (FREQS, FREQS), 1) - FREQS // 2

    turned = (kz + FREQS) % FREQS - FREQS // 2

    def weigh(row, _):
        ky, ky_outer = ky_of(chip, row), ky_of(chip, 7)
        outside = (row == 6) & (ky * ky + kz * kz >= FREQS * FREQS // 4)
        square = jnp.where(
            outside, ky_outer * ky_outer + turned * turned, ky * ky + kz * kz
        ) + kx * kx
        inside = (square > 0) & (square < FREQS * FREQS // 4)
        safe = jnp.where(inside, square, 1).astype(F32)
        scale = cell_length**2 / math.pi / float(POINTS) ** 3
        weights[row] = jnp.where(inside, jnp.float32(scale) / safe, jnp.float32(0.0))
        return 0

    row_in = (kx + FREQS // 2) % 8
    ky = ky_of((kx + FREQS // 2) // 8, row_in)
    in_disc = ky * ky + kz * kz < FREQS * FREQS // 4
    take_outer = (row_in == 6) & jnp.logical_not(in_disc)

    lax.fori_loop(0, SENT, weigh, 0)

    for bit in range(5):
        pl.semaphore_signal(
            met.at[bit], inc=1, device_id=(band, flipped(bit)), device_id_type=MESH
        )
        pl.semaphore_wait(met.at[bit], 1)

    load.wait()
    for table in tables:
        table.wait()
    gathered[band] = own[band]
    part = gathered.at[pl.ds(0, 7)]
    pltpu.make_async_copy(part, part, spread_recv.at[0]).wait()
    for o in range(2):
        slot = 0
        for s in range(1, 8):
            slot = jnp.where(info_ref[s] == info_ref[8 + o], s, slot)
        held[o, band] = gathered[slot]

    def relay(o, depth):
        table, trees, depths, _ = SCHEMES[o]
        for i, (first, count) in enumerate(table):
            for relative in range(8):
                if depths[i][relative] != depth:
                    continue
                origin = source(relative)
                part = held.at[o, origin, pl.ds(first, count)]
                if depth:
                    pltpu.make_async_copy(part, part, tree_recv.at[o, origin, i]).wait()
                for way in range(3):
                    if relative in trees[i][way]:
                        pltpu.make_async_remote_copy(
                            src_ref=part, dst_ref=part,
                            send_sem=tree_send.at[o], recv_sem=tree_recv.at[o, origin, i],
                            device_id=(neighbours[way], place), device_id_type=MESH,
                        ).start()

    def plane(o, k):
        return source(sum(jnp.where(k == n, relative, 0) for n, relative in enumerate(SCHEMES[o][3])))

    def forward(o, k):
        p = plane(o, k)
        density = held[o, p] * own[p]
        level = jnp.sum(density, keepdims=True) * (1.0 / POINTS**2)
        high, low = split(density - level)
        along_z = quarters(dot(jnp.concatenate([high, low], axis=0), tall_ref[...]))
        high, low = split(along_z)
        along_y = quarters(dot(wide_y[...], jnp.concatenate([high, low], axis=1)))
        along_y = along_y + jnp.where((kx == 0) & (kz == 0), level * float(POINTS**2), 0.0)
        outer = pltpu.roll(pltpu.roll(along_y, FREQS - 1, 0), FREQS // 2, 1)
        along_y = jnp.where(take_outer, outer, along_y)
        ahead[o, :, k] = along_y.reshape(CHIPS, 8, FREQS)

    def send_ahead(o, first, count):
        def ends(there):
            source = ahead.at[o, there, pl.ds(first, count), pl.ds(0, SENT)]
            return source, arrived.at[pl.ds(place * PLANES + first, count), pl.ds(0, SENT)]

        def send(there):
            source, target = ends(there)
            pltpu.make_async_remote_copy(
                src_ref=source, dst_ref=target,
                send_sem=ahead_send.at[o], recv_sem=ahead_recv.at[0],
                device_id=(band, there * 2 + o), device_id_type=MESH,
            ).start()

        def one(k, _):
            send((chip + k) % CHIPS)
            return 0

        @pl.when(core == o)
        def _():
            source, target = ends(chip)
            pltpu.make_async_copy(source, target, ahead_recv.at[0]).start()

        @pl.when(core != o)
        def _():
            send(chip)

        lax.fori_loop(1, CHIPS, one, 0, unroll=UNROLL)

    def transform(o, first, last):
        def one(k, _):
            forward(o, k)
            return 0

        lax.fori_loop(first, last, one, 0)
        send_ahead(o, first, last - first)


    def middle(o):
        @pl.when(core == o)
        def _():
            landed = arrived.at[:, pl.ds(0, SENT)]
            pltpu.make_async_copy(landed, landed, ahead_recv.at[0]).wait()

            def one(row, _):
                column = arrived[:, pl.ds(row, 1), :].reshape(POINTS, FREQS)
                level = jnp.sum(column, axis=0, keepdims=True) * (1.0 / POINTS)
                high, low = split(column - level)
                along_x = quarters(dot(wide_x[...], jnp.concatenate([high, low], axis=1)))
                along_x = along_x + jnp.where(kx == 0, level * float(POINTS), 0.0)
                high, low = split(along_x * weights[row])
                pair = jnp.concatenate([high, low], axis=1)
                both = dot(tall_x[...], jnp.concatenate([pair, pair], axis=0))
                back[:, pl.ds(row, 1), :] = (both[:, :FREQS] + both[:, FREQS:]).reshape(POINTS, 1, FREQS)
                return 0

            lax.fori_loop(0, SENT, one, 0, unroll=True)
    def group(o, h):
        size = PLANES // RETURNS[o]
        return h * size, size

    def give_back(o, h):
        first, size = group(o, h)

        @pl.when(core == o)
        def _():
            def ends(there):
                source = back.at[pl.ds(there * PLANES + first, size), pl.ds(0, SENT)]
                return source, restored.at[o, chip, pl.ds(first, size), pl.ds(0, SENT)]

            def one(k, _):
                there = (place + k) % 32
                source, target = ends(there)
                pltpu.make_async_remote_copy(
                    src_ref=source, dst_ref=target,
                    send_sem=back_send.at[0], recv_sem=back_recv.at[o, h],
                    device_id=(band, there), device_id_type=MESH,
                ).start()
                return 0

            source, target = ends(place)
            pltpu.make_async_copy(source, target, back_recv.at[o, h]).start()
            lax.fori_loop(1, 32, one, 0, unroll=UNROLL)

    def backward(o, k):
        coeffs = restored[o, :, k].reshape(FREQS, FREQS)
        outer = pltpu.roll(pltpu.roll(coeffs, 1, 0), FREQS // 2, 1)
        coeffs = jnp.where(in_disc, jnp.where(row_in == 7, outer, coeffs), 0.0)
        high, low = split(coeffs)
        pair = jnp.concatenate([high, low], axis=1)
        both = dot(tall_y[...], jnp.concatenate([pair, pair], axis=0))
        high, low = split(both[:, :FREQS] + both[:, FREQS:])
        field = dot(jnp.concatenate([high, low], axis=1), jnp.concatenate([wide_ref[:FREQS], wide_ref[:FREQS]], axis=0))
        field = field + dot(high, wide_ref[FREQS:])
        return held[o, plane(o, k)] * field

    for name, *numbers in PROGRAM:
        {"r": relay, "t": transform, "m": middle, "b": give_back}[name](*numbers)

    for h in range(RETURNS[0]):
        first, size = group(0, h)
        part = restored.at[0, :, pl.ds(first, size), pl.ds(0, SENT)]
        pltpu.make_async_copy(part, part, back_recv.at[0, h]).wait()

        def one(k, _):
            partial[plane(0, k)] = backward(0, k)
            return 0

        lax.fori_loop(first, first + size, one, 0)
    for h in range(RETURNS[1]):
        first, size = group(1, h)
        part = restored.at[1, :, pl.ds(first, size), pl.ds(0, SENT)]
        pltpu.make_async_copy(part, part, back_recv.at[1, h]).wait()

        def one(k, _):
            p = plane(1, k)
            out_ref[0, p] = -(partial[p] + backward(1, k))
            return 0

        lax.fori_loop(first, first + size, one, 0)

    part = gathered.at[pl.ds(0, 7)]
    pltpu.make_async_copy(part, part, spread_send.at[0]).wait()
    for o in range(2):
        part = held.at[o, pl.ds(0, 7)]
        pltpu.make_async_copy(part, part, tree_send.at[o]).wait()

        @pl.when(core == o)
        def _():
            part = ahead.at[o, pl.ds(0, CHIPS - 1), :, pl.ds(0, SENT)]
            pltpu.make_async_copy(part, part, ahead_send.at[o]).wait()

        @pl.when(core != o)
        def _():
            part = ahead.at[o, :, :, pl.ds(0, SENT)]
            pltpu.make_async_copy(part, part, ahead_send.at[o]).wait()

    part = back.at[pl.ds(0, 31 * PLANES), pl.ds(0, SENT)]
    pltpu.make_async_copy(part, part, back_send.at[0]).wait()


def cas_tables(freqs):
    positions = np.arange(POINTS)[:, None] * freqs[None, :] % POINTS
    angles = positions * (2.0 * math.pi / POINTS)
    cas = np.cos(angles) + np.sin(angles)
    high = cas.astype(ml_dtypes.bfloat16)
    low = (cas - high.astype(np.float64)).astype(ml_dtypes.bfloat16)
    tall = np.concatenate([high, low], axis=1)
    wide = np.concatenate([high.T, low.T], axis=0)
    return tall, wide


def constants():
    tall, wide = cas_tables(np.arange(FREQS) - FREQS // 2)
    ky = []
    for block in range(CHIPS):
        ky += [6 * block + row - 48 for row in range(6)]
        ky += [48 + block, 63 - block] if block < 8 else [-40 - block, block - 71]
    ky[0] = -64
    tall_y, wide_y = cas_tables(np.array(ky))
    tall_x, wide_x = [], []
    for o, band in itertools.product(range(2), range(8)):
        planes = [((band // 2 - r // 2) % 4) * 2 + (band + r) % 2 for r in SCHEMES[o][3]]
        rows = np.concatenate([block * PLANES + np.array(planes) for block in range(POINTS // PLANES)])
        tall_x.append(tall[rows])
        wide_x.append(wide[:, rows])
    return np.stack(tall_x + wide_x + [tall, wide, tall_y, wide_y])


def exchange():
    dma = pltpu.SemaphoreType.DMA
    return pl.pallas_call(
        kernel,
        out_shape=jax.ShapeDtypeStruct((1, PLANES, POINTS, POINTS), F32),
        in_specs=[pl.BlockSpec(memory_space=pl.ANY)] * 3,
        out_specs=pl.BlockSpec(memory_space=pltpu.VMEM),
        scratch_shapes=[
            pltpu.VMEM((POINTS, 2 * FREQS), BF16),
            pltpu.VMEM((2 * FREQS, POINTS), BF16),
            pltpu.VMEM((POINTS, 2 * FREQS), BF16),
            pltpu.VMEM((2 * FREQS, POINTS), BF16),
            pltpu.VMEM((POINTS, 2 * FREQS), BF16),
            pltpu.VMEM((2 * FREQS, POINTS), BF16),
            pltpu.VMEM((8, POINTS, POINTS), F32),
            pltpu.VMEM((2, PLANES, POINTS, POINTS), F32),
            pltpu.VMEM((PLANES, POINTS, POINTS), F32),
            pltpu.VMEM((2, CHIPS, PLANES, 8, FREQS), F32),
            pltpu.VMEM((POINTS, 8, FREQS), F32),
            pltpu.VMEM((POINTS, 8, FREQS), F32),
            pltpu.VMEM((2, CHIPS, PLANES, 8, FREQS), F32),
            pltpu.VMEM((8, FREQS, FREQS), F32),
            pltpu.VMEM((PLANES, POINTS, POINTS), F32),
            pltpu.SMEM((10,), jnp.int32), dma((8,)), pltpu.SemaphoreType.REGULAR((5,)), dma((1,)), dma((1,)), dma((2,)), dma((2, 8, 6)),
            dma((2,)), dma((1,)), dma((1,)), dma((2, max(RETURNS))),
        ],
        compiler_params=pltpu.CompilerParams(
            collective_id=0, has_side_effects=True, vmem_limit_bytes=VMEM_MIB << 20
        ),
    )


def per_device(orbitals, band_ids, owners):
    return exchange()(orbitals, jnp.concatenate([band_ids, owners]), jnp.asarray(constants()))


def solution(mesh):
    placed = (P("band", "fft", None, None), P(), P())
    return jax.shard_map(
        per_device,
        mesh=mesh,
        in_specs=placed,
        out_specs=P("band", "fft", None, None),
        check_vma=False,
    )
```

```python
import itertools
import math

import jax
import jax.numpy as jnp
import ml_dtypes
import numpy as np
from jax import lax
from jax.experimental import pallas as pl
from jax.experimental.pallas import tpu as pltpu
from jax.sharding import PartitionSpec as P

MESH = pl.DeviceIdType.MESH
F32 = jnp.float32
BF16 = jnp.bfloat16
cell_length = 46.9

POINTS = 256
FREQS = 128
PLANES = 8
CHIPS = 16
VMEM_MIB = 50
T_TREES = (
    ((0, 2, 4, 5), (3,), (2, 4)),
    ((7,), (0, 6, 4, 7, 5), (6,)),
    ((1, 3), (1,), (0, 3, 5, 7)),
)
T_DEPTHS = ((0, 3, 1, 2, 2, 3, 3, 4), (0, 3, 3, 4, 2, 3, 1, 2), (0, 1, 3, 2, 4, 3, 3, 2))
T_ORDER = (0, 1, 2, 5, 6, 3, 4, 7)
W = (((0, 48), (48, 40), (88, 40), (128, 40), (168, 48), (216, 40)), T_TREES * 2, T_DEPTHS * 2, T_ORDER)
SCHEMES = (W, W)
PROGRAM = (
    ("p", 0), ("r", 0, 0, 0), ("r", 1, 0, 0), ("p", 1), ("r", 0, 0, 1), ("r", 1, 0, 1), ("r", 0, 1),
    ("r", 0, 2), ("r", 1, 1), ("r", 0, 3), ("t", 0, 0, 5), ("r", 1, 2), ("r", 0, 4), ("t", 0, 5, 8),
    ("r", 1, 3), ("t", 1, 0, 5), ("r", 1, 4), ("t", 1, 5, 8), ("m", 0), ("b", 0, 0), ("b", 0, 1), ("m", 1),
    ("b", 1, 0), ("b", 1, 1), ("b", 1, 2), ("b", 1, 3),
)


SENT = 7
UNROLL = True
RETURNS = (2, 4)


def ky_of(block, row):
    plain = 6 * block + row - 48
    plain = jnp.where(plain == -48, -64, plain)
    inner = jnp.where(block < 8, 48 + block, -40 - block)
    outer = jnp.where(block < 8, 63 - block, block - 71)
    return jnp.where(row < 6, plain, jnp.where(row == 6, inner, outer))


def split(value):
    high = value.astype(BF16)
    return high, (value - high.astype(F32)).astype(BF16)


def dot(left, right):
    return jnp.dot(left, right, preferred_element_type=F32)


def quarters(value):
    rows, columns = value.shape[0] // 2, value.shape[1] // 2
    small = (value[:rows, columns:] + value[rows:, :columns]) + value[rows:, columns:]
    return value[:rows, :columns] + small


def kernel(
    orb_ref, info_in, tables_in, out_ref,
    tall_ref, wide_ref, tall_y, wide_y, tall_x, wide_x, gathered_0, gathered_1, held, own, ahead, arrived, back, restored, weights, partial,
    info_ref, in_sem, met, spread_send, spread_recv, tree_send, tree_recv, ahead_send, ahead_recv, back_send, back_recv,
):
    band = lax.axis_index("band")
    place = lax.axis_index("fft")
    my_x, my_y = band // 2, band % 2
    chip, core = place // 2, place % 2

    def band_at(x, y):
        return ((my_x + x) % 4) * 2 + (my_y + y) % 2

    def source(relative):
        return band_at(4 - relative // 2, relative % 2)

    def flipped(bit):
        step = 1 << bit
        return place + step - 2 * step * ((place // step) % 2)

    neighbours = (band_at(1, 0), band_at(3, 0), band_at(0, 1))

    load = pltpu.make_async_copy(orb_ref.at[0], own, in_sem.at[0])
    load.start()
    tables = (
        pltpu.make_async_copy(info_in, info_ref, in_sem.at[7]),
        pltpu.make_async_copy(tables_in.at[32], tall_ref, in_sem.at[1]),
        pltpu.make_async_copy(tables_in.at[33], wide_ref, in_sem.at[2]),
        pltpu.make_async_copy(tables_in.at[34], tall_y, in_sem.at[5]),
        pltpu.make_async_copy(tables_in.at[35], wide_y, in_sem.at[6]),
        pltpu.make_async_copy(tables_in.at[core * 8 + band], tall_x, in_sem.at[3]),
        pltpu.make_async_copy(tables_in.at[core * 8 + band + 16], wide_x, in_sem.at[4]),
    )
    for table in tables:
        table.start()
    barrier = pltpu.get_barrier_semaphore()
    for k in range(1, 8):
        pl.semaphore_signal(
            barrier, inc=1, device_id=((band + k) % 8, place), device_id_type=MESH
        )

    for bit in range(5):
        pl.semaphore_signal(
            barrier, inc=1, device_id=(band, flipped(bit)), device_id_type=MESH
        )
    pl.semaphore_wait(barrier, 12)
    gathered = (gathered_0, gathered_1)
    half_rows = POINTS // 2
    for half in range(2):
        rows = pl.ds(half * half_rows, half_rows)
        for relative in (4, 5, 2, 6, 3, 7, 1):
            there = source(relative)
            pltpu.make_async_remote_copy(
                src_ref=orb_ref.at[0, there, rows], dst_ref=gathered[half].at[band],
                send_sem=spread_send.at[half], recv_sem=spread_recv.at[half],
                device_id=(there, place), device_id_type=MESH,
            ).start()

    kx = lax.broadcasted_iota(jnp.int32, (FREQS, FREQS), 0) - FREQS // 2
    kz = lax.broadcasted_iota(jnp.int32, (FREQS, FREQS), 1) - FREQS // 2

    turned = (kz + FREQS) % FREQS - FREQS // 2

    def weigh(row, _):
        ky, ky_outer = ky_of(chip, row), ky_of(chip, 7)
        outside = (row == 6) & (ky * ky + kz * kz >= FREQS * FREQS // 4)
        square = jnp.where(
            outside, ky_outer * ky_outer + turned * turned, ky * ky + kz * kz
        ) + kx * kx
        inside = (square > 0) & (square < FREQS * FREQS // 4)
        safe = jnp.where(inside, square, 1).astype(F32)
        scale = cell_length**2 / math.pi / float(POINTS) ** 3
        weights[row] = jnp.where(inside, jnp.float32(scale) / safe, jnp.float32(0.0))
        return 0

    row_in = (kx + FREQS // 2) % 8
    ky = ky_of((kx + FREQS // 2) // 8, row_in)
    in_disc = ky * ky + kz * kz < FREQS * FREQS // 4
    take_outer = (row_in == 6) & jnp.logical_not(in_disc)

    lax.fori_loop(0, SENT, weigh, 0)

    for bit in range(5):
        pl.semaphore_signal(
            met.at[bit], inc=1, device_id=(band, flipped(bit)), device_id_type=MESH
        )
        pl.semaphore_wait(met.at[bit], 1)

    load.wait()
    for table in tables:
        table.wait()
    slots = []
    for o in range(2):
        slot = 0
        for s in range(1, 8):
            slot = jnp.where(info_ref[s] == info_ref[8 + o], s, slot)
        slots.append(slot)

    def pick(half):
        rows = pl.ds(half * half_rows, half_rows)
        gathered[half][band] = own[band, rows]
        part = gathered[half].at[pl.ds(0, 7)]
        pltpu.make_async_copy(part, part, spread_recv.at[half]).wait()
        for o in range(2):
            held[o, band, rows] = gathered[half][slots[o]]

    def relay(o, depth, *halves):
        table, trees, depths, _ = SCHEMES[o]
        for i, (first, count) in enumerate(table):
            if halves and first // half_rows not in halves:
                continue
            for relative in range(8):
                if depths[i][relative] != depth:
                    continue
                origin = source(relative)
                part = held.at[o, origin, pl.ds(first, count)]
                if depth:
                    pltpu.make_async_copy(part, part, tree_recv.at[o, origin, i]).wait()
                for way in range(3):
                    if relative in trees[i][way]:
                        pltpu.make_async_remote_copy(
                            src_ref=part, dst_ref=part,
                            send_sem=tree_send.at[o], recv_sem=tree_recv.at[o, origin, i],
                            device_id=(neighbours[way], place), device_id_type=MESH,
                        ).start()

    def plane(o, k):
        return source(sum(jnp.where(k == n, relative, 0) for n, relative in enumerate(SCHEMES[o][3])))

    def forward(o, k):
        p = plane(o, k)
        density = held[o, p] * own[p]
        level = jnp.sum(density, keepdims=True) * (1.0 / POINTS**2)
        high, low = split(density - level)
        along_z = quarters(dot(jnp.concatenate([high, low], axis=0), tall_ref[...]))
        high, low = split(along_z)
        along_y = quarters(dot(wide_y[...], jnp.concatenate([high, low], axis=1)))
        along_y = along_y + jnp.where((kx == 0) & (kz == 0), level * float(POINTS**2), 0.0)
        outer = pltpu.roll(pltpu.roll(along_y, FREQS - 1, 0), FREQS // 2, 1)
        along_y = jnp.where(take_outer, outer, along_y)
        ahead[o, :, k] = along_y.reshape(CHIPS, 8, FREQS)

    def send_ahead(o, first, count):
        def ends(there):
            source = ahead.at[o, there, pl.ds(first, count), pl.ds(0, SENT)]
            return source, arrived.at[pl.ds(place * PLANES + first, count), pl.ds(0, SENT)]

        def send(there):
            source, target = ends(there)
            pltpu.make_async_remote_copy(
                src_ref=source, dst_ref=target,
                send_sem=ahead_send.at[o], recv_sem=ahead_recv.at[0],
                device_id=(band, there * 2 + o), device_id_type=MESH,
            ).start()

        def one(k, _):
            send((chip + k) % CHIPS)
            return 0

        @pl.when(core == o)
        def _():
            source, target = ends(chip)
            pltpu.make_async_copy(source, target, ahead_recv.at[0]).start()

        @pl.when(core != o)
        def _():
            send(chip)

        lax.fori_loop(1, CHIPS, one, 0, unroll=UNROLL)

    def transform(o, first, last):
        def one(k, _):
            forward(o, k)
            return 0

        lax.fori_loop(first, last, one, 0)
        send_ahead(o, first, last - first)


    def middle(o):
        @pl.when(core == o)
        def _():
            landed = arrived.at[:, pl.ds(0, SENT)]
            pltpu.make_async_copy(landed, landed, ahead_recv.at[0]).wait()

            def one(row, _):
                column = arrived[:, pl.ds(row, 1), :].reshape(POINTS, FREQS)
                level = jnp.sum(column, axis=0, keepdims=True) * (1.0 / POINTS)
                high, low = split(column - level)
                along_x = quarters(dot(wide_x[...], jnp.concatenate([high, low], axis=1)))
                along_x = along_x + jnp.where(kx == 0, level * float(POINTS), 0.0)
                high, low = split(along_x * weights[row])
                pair = jnp.concatenate([high, low], axis=1)
                both = dot(tall_x[...], jnp.concatenate([pair, pair], axis=0))
                back[:, pl.ds(row, 1), :] = (both[:, :FREQS] + both[:, FREQS:]).reshape(POINTS, 1, FREQS)
                return 0

            lax.fori_loop(0, SENT, one, 0, unroll=True)
    def group(o, h):
        size = PLANES // RETURNS[o]
        return h * size, size

    def give_back(o, h):
        first, size = group(o, h)

        @pl.when(core == o)
        def _():
            def ends(there):
                source = back.at[pl.ds(there * PLANES + first, size), pl.ds(0, SENT)]
                return source, restored.at[o, chip, pl.ds(first, size), pl.ds(0, SENT)]

            def one(k, _):
                there = (place + k) % 32
                source, target = ends(there)
                pltpu.make_async_remote_copy(
                    src_ref=source, dst_ref=target,
                    send_sem=back_send.at[0], recv_sem=back_recv.at[o, h],
                    device_id=(band, there), device_id_type=MESH,
                ).start()
                return 0

            source, target = ends(place)
            pltpu.make_async_copy(source, target, back_recv.at[o, h]).start()
            lax.fori_loop(1, 32, one, 0, unroll=UNROLL)

    def backward(o, k):
        coeffs = restored[o, :, k].reshape(FREQS, FREQS)
        outer = pltpu.roll(pltpu.roll(coeffs, 1, 0), FREQS // 2, 1)
        coeffs = jnp.where(in_disc, jnp.where(row_in == 7, outer, coeffs), 0.0)
        high, low = split(coeffs)
        pair = jnp.concatenate([high, low], axis=1)
        both = dot(tall_y[...], jnp.concatenate([pair, pair], axis=0))
        high, low = split(both[:, :FREQS] + both[:, FREQS:])
        field = dot(jnp.concatenate([high, low], axis=1), jnp.concatenate([wide_ref[:FREQS], wide_ref[:FREQS]], axis=0))
        field = field + dot(high, wide_ref[FREQS:])
        return held[o, plane(o, k)] * field

    for name, *numbers in PROGRAM:
        {"r": relay, "p": pick, "t": transform, "m": middle, "b": give_back}[name](*numbers)

    for h in range(RETURNS[0]):
        first, size = group(0, h)
        part = restored.at[0, :, pl.ds(first, size), pl.ds(0, SENT)]
        pltpu.make_async_copy(part, part, back_recv.at[0, h]).wait()

        def one(k, _):
            partial[plane(0, k)] = backward(0, k)
            return 0

        lax.fori_loop(first, first + size, one, 0)
    for h in range(RETURNS[1]):
        first, size = group(1, h)
        part = restored.at[1, :, pl.ds(first, size), pl.ds(0, SENT)]
        pltpu.make_async_copy(part, part, back_recv.at[1, h]).wait()

        def one(k, _):
            p = plane(1, k)
            out_ref[0, p] = -(partial[p] + backward(1, k))
            return 0

        lax.fori_loop(first, first + size, one, 0)

    for half in range(2):
        part = gathered[half].at[pl.ds(0, 7)]
        pltpu.make_async_copy(part, part, spread_send.at[half]).wait()
    for o in range(2):
        part = held.at[o, pl.ds(0, 7)]
        pltpu.make_async_copy(part, part, tree_send.at[o]).wait()

        @pl.when(core == o)
        def _():
            part = ahead.at[o, pl.ds(0, CHIPS - 1), :, pl.ds(0, SENT)]
            pltpu.make_async_copy(part, part, ahead_send.at[o]).wait()

        @pl.when(core != o)
        def _():
            part = ahead.at[o, :, :, pl.ds(0, SENT)]
            pltpu.make_async_copy(part, part, ahead_send.at[o]).wait()

    part = back.at[pl.ds(0, 31 * PLANES), pl.ds(0, SENT)]
    pltpu.make_async_copy(part, part, back_send.at[0]).wait()


def cas_tables(freqs):
    positions = np.arange(POINTS)[:, None] * freqs[None, :] % POINTS
    angles = positions * (2.0 * math.pi / POINTS)
    cas = np.cos(angles) + np.sin(angles)
    high = cas.astype(ml_dtypes.bfloat16)
    low = (cas - high.astype(np.float64)).astype(ml_dtypes.bfloat16)
    tall = np.concatenate([high, low], axis=1)
    wide = np.concatenate([high.T, low.T], axis=0)
    return tall, wide


def constants():
    tall, wide = cas_tables(np.arange(FREQS) - FREQS // 2)
    ky = []
    for block in range(CHIPS):
        ky += [6 * block + row - 48 for row in range(6)]
        ky += [48 + block, 63 - block] if block < 8 else [-40 - block, block - 71]
    ky[0] = -64
    tall_y, wide_y = cas_tables(np.array(ky))
    tall_x, wide_x = [], []
    for o, band in itertools.product(range(2), range(8)):
        planes = [((band // 2 - r // 2) % 4) * 2 + (band + r) % 2 for r in SCHEMES[o][3]]
        rows = np.concatenate([block * PLANES + np.array(planes) for block in range(POINTS // PLANES)])
        tall_x.append(tall[rows])
        wide_x.append(wide[:, rows])
    return np.stack(tall_x + wide_x + [tall, wide, tall_y, wide_y])


def exchange():
    dma = pltpu.SemaphoreType.DMA
    return pl.pallas_call(
        kernel,
        out_shape=jax.ShapeDtypeStruct((1, PLANES, POINTS, POINTS), F32),
        in_specs=[pl.BlockSpec(memory_space=pl.ANY)] * 3,
        out_specs=pl.BlockSpec(memory_space=pltpu.VMEM),
        scratch_shapes=[
            pltpu.VMEM((POINTS, 2 * FREQS), BF16),
            pltpu.VMEM((2 * FREQS, POINTS), BF16),
            pltpu.VMEM((POINTS, 2 * FREQS), BF16),
            pltpu.VMEM((2 * FREQS, POINTS), BF16),
            pltpu.VMEM((POINTS, 2 * FREQS), BF16),
            pltpu.VMEM((2 * FREQS, POINTS), BF16),
            pltpu.VMEM((8, POINTS // 2, POINTS), F32),
            pltpu.VMEM((8, POINTS // 2, POINTS), F32),
            pltpu.VMEM((2, PLANES, POINTS, POINTS), F32),
            pltpu.VMEM((PLANES, POINTS, POINTS), F32),
            pltpu.VMEM((2, CHIPS, PLANES, 8, FREQS), F32),
            pltpu.VMEM((POINTS, 8, FREQS), F32),
            pltpu.VMEM((POINTS, 8, FREQS), F32),
            pltpu.VMEM((2, CHIPS, PLANES, 8, FREQS), F32),
            pltpu.VMEM((8, FREQS, FREQS), F32),
            pltpu.VMEM((PLANES, POINTS, POINTS), F32),
            pltpu.SMEM((10,), jnp.int32), dma((8,)), pltpu.SemaphoreType.REGULAR((5,)), dma((2,)), dma((2,)), dma((2,)), dma((2, 8, 6)),
            dma((2,)), dma((1,)), dma((1,)), dma((2, max(RETURNS))),
        ],
        compiler_params=pltpu.CompilerParams(
            collective_id=0, has_side_effects=True, vmem_limit_bytes=VMEM_MIB << 20
        ),
    )


def per_device(orbitals, band_ids, owners):
    return exchange()(orbitals, jnp.concatenate([band_ids, owners]), jnp.asarray(constants()))


def solution(mesh):
    placed = (P("band", "fft", None, None), P(), P())
    return jax.shard_map(
        per_device,
        mesh=mesh,
        in_specs=placed,
        out_specs=P("band", "fft", None, None),
        check_vma=False,
    )
```

```python
import itertools
import math

import jax
import jax.numpy as jnp
import ml_dtypes
import numpy as np
from jax import lax
from jax.experimental import pallas as pl
from jax.experimental.pallas import tpu as pltpu
from jax.sharding import PartitionSpec as P

MESH = pl.DeviceIdType.MESH
F32 = jnp.float32
BF16 = jnp.bfloat16
cell_length = 46.9

POINTS = 256
FREQS = 128
PLANES = 8
CHIPS = 16
VMEM_MIB = 50
T_TREES = (
    ((0, 2, 4, 5), (3,), (2, 4)),
    ((7,), (0, 6, 4, 7, 5), (6,)),
    ((1, 3), (1,), (0, 3, 5, 7)),
)
T_DEPTHS = ((0, 3, 1, 2, 2, 3, 3, 4), (0, 3, 3, 4, 2, 3, 1, 2), (0, 1, 3, 2, 4, 3, 3, 2))
T_ORDER = (0, 1, 2, 5, 6, 3, 4, 7)
W = (((0, 48), (48, 40), (88, 40), (128, 40), (168, 48), (216, 40)), T_TREES * 2, T_DEPTHS * 2, T_ORDER)
SCHEMES = (W, W)
PROGRAM = (
    ("p", 0), ("r", 0, 0, 0), ("r", 1, 0, 0), ("r", 0, 1, 0), ("p", 1), ("r", 0, 0, 1), ("r", 1, 0, 1),
    ("r", 0, 1, 1), ("r", 0, 2), ("r", 1, 1), ("r", 0, 3), ("t", 0, 0, 5), ("r", 1, 2), ("r", 0, 4),
    ("t", 0, 5, 8), ("r", 1, 3), ("t", 1, 0, 5), ("r", 1, 4), ("t", 1, 5, 8), ("m", 0), ("b", 0, 0),
    ("b", 0, 1), ("m", 1), ("b", 1, 0), ("b", 1, 1), ("b", 1, 2), ("b", 1, 3),
)


SENT = 7
UNROLL = True
RETURNS = (2, 4)


def ky_of(block, row):
    plain = 6 * block + row - 48
    plain = jnp.where(plain == -48, -64, plain)
    inner = jnp.where(block < 8, 48 + block, -40 - block)
    outer = jnp.where(block < 8, 63 - block, block - 71)
    return jnp.where(row < 6, plain, jnp.where(row == 6, inner, outer))


def split(value):
    high = value.astype(BF16)
    return high, (value - high.astype(F32)).astype(BF16)


def dot(left, right):
    return jnp.dot(left, right, preferred_element_type=F32)


def quarters(value):
    rows, columns = value.shape[0] // 2, value.shape[1] // 2
    small = (value[:rows, columns:] + value[rows:, :columns]) + value[rows:, columns:]
    return value[:rows, :columns] + small


def kernel(
    orb_ref, info_in, tables_in, out_ref,
    tall_ref, wide_ref, tall_y, wide_y, tall_x, wide_x, gathered_0, gathered_1, held, own, ahead, arrived, back, restored, weights, partial,
    info_ref, in_sem, met, spread_send, spread_recv, tree_send, tree_recv, ahead_send, ahead_recv, back_send, back_recv,
):
    band = lax.axis_index("band")
    place = lax.axis_index("fft")
    my_x, my_y = band // 2, band % 2
    chip, core = place // 2, place % 2

    def band_at(x, y):
        return ((my_x + x) % 4) * 2 + (my_y + y) % 2

    def source(relative):
        return band_at(4 - relative // 2, relative % 2)

    def flipped(bit):
        step = 1 << bit
        return place + step - 2 * step * ((place // step) % 2)

    neighbours = (band_at(1, 0), band_at(3, 0), band_at(0, 1))

    load = pltpu.make_async_copy(orb_ref.at[0], own, in_sem.at[0])
    load.start()
    tables = (
        pltpu.make_async_copy(info_in, info_ref, in_sem.at[7]),
        pltpu.make_async_copy(tables_in.at[32], tall_ref, in_sem.at[1]),
        pltpu.make_async_copy(tables_in.at[33], wide_ref, in_sem.at[2]),
        pltpu.make_async_copy(tables_in.at[34], tall_y, in_sem.at[5]),
        pltpu.make_async_copy(tables_in.at[35], wide_y, in_sem.at[6]),
        pltpu.make_async_copy(tables_in.at[core * 8 + band], tall_x, in_sem.at[3]),
        pltpu.make_async_copy(tables_in.at[core * 8 + band + 16], wide_x, in_sem.at[4]),
    )
    for table in tables:
        table.start()
    barrier = pltpu.get_barrier_semaphore()
    for k in range(1, 8):
        pl.semaphore_signal(
            barrier, inc=1, device_id=((band + k) % 8, place), device_id_type=MESH
        )

    for bit in range(5):
        pl.semaphore_signal(
            barrier, inc=1, device_id=(band, flipped(bit)), device_id_type=MESH
        )
    pl.semaphore_wait(barrier, 12)
    gathered = (gathered_0, gathered_1)
    half_rows = POINTS // 2
    for half in range(2):
        rows = pl.ds(half * half_rows, half_rows)
        for relative in (4, 5, 2, 6, 3, 7, 1):
            there = source(relative)
            pltpu.make_async_remote_copy(
                src_ref=orb_ref.at[0, there, rows], dst_ref=gathered[half].at[band],
                send_sem=spread_send.at[half], recv_sem=spread_recv.at[half],
                device_id=(there, place), device_id_type=MESH,
            ).start()

    kx = lax.broadcasted_iota(jnp.int32, (FREQS, FREQS), 0) - FREQS // 2
    kz = lax.broadcasted_iota(jnp.int32, (FREQS, FREQS), 1) - FREQS // 2

    turned = (kz + FREQS) % FREQS - FREQS // 2

    def weigh(row, _):
        ky, ky_outer = ky_of(chip, row), ky_of(chip, 7)
        outside = (row == 6) & (ky * ky + kz * kz >= FREQS * FREQS // 4)
        square = jnp.where(
            outside, ky_outer * ky_outer + turned * turned, ky * ky + kz * kz
        ) + kx * kx
        inside = (square > 0) & (square < FREQS * FREQS // 4)
        safe = jnp.where(inside, square, 1).astype(F32)
        scale = cell_length**2 / math.pi / float(POINTS) ** 3
        weights[row] = jnp.where(inside, jnp.float32(scale) / safe, jnp.float32(0.0))
        return 0

    row_in = (kx + FREQS // 2) % 8
    ky = ky_of((kx + FREQS // 2) // 8, row_in)
    in_disc = ky * ky + kz * kz < FREQS * FREQS // 4
    take_outer = (row_in == 6) & jnp.logical_not(in_disc)

    lax.fori_loop(0, SENT, weigh, 0)

    for bit in range(5):
        pl.semaphore_signal(
            met.at[bit], inc=1, device_id=(band, flipped(bit)), device_id_type=MESH
        )
        pl.semaphore_wait(met.at[bit], 1)

    load.wait()
    for table in tables:
        table.wait()
    slots = []
    for o in range(2):
        slot = 0
        for s in range(1, 8):
            slot = jnp.where(info_ref[s] == info_ref[8 + o], s, slot)
        slots.append(slot)

    def pick(half):
        rows = pl.ds(half * half_rows, half_rows)
        gathered[half][band] = own[band, rows]
        part = gathered[half].at[pl.ds(0, 7)]
        pltpu.make_async_copy(part, part, spread_recv.at[half]).wait()
        for o in range(2):
            held[o, band, rows] = gathered[half][slots[o]]

    def relay(o, depth, *halves):
        table, trees, depths, _ = SCHEMES[o]
        for i, (first, count) in enumerate(table):
            if halves and first // half_rows not in halves:
                continue
            for relative in range(8):
                if depths[i][relative] != depth:
                    continue
                origin = source(relative)
                part = held.at[o, origin, pl.ds(first, count)]
                if depth:
                    pltpu.make_async_copy(part, part, tree_recv.at[o, origin, i]).wait()
                for way in range(3):
                    if relative in trees[i][way]:
                        pltpu.make_async_remote_copy(
                            src_ref=part, dst_ref=part,
                            send_sem=tree_send.at[o], recv_sem=tree_recv.at[o, origin, i],
                            device_id=(neighbours[way], place), device_id_type=MESH,
                        ).start()

    def plane(o, k):
        return source(sum(jnp.where(k == n, relative, 0) for n, relative in enumerate(SCHEMES[o][3])))

    def forward(o, k):
        p = plane(o, k)
        density = held[o, p] * own[p]
        level = jnp.sum(density, keepdims=True) * (1.0 / POINTS**2)
        high, low = split(density - level)
        along_z = quarters(dot(jnp.concatenate([high, low], axis=0), tall_ref[...]))
        high, low = split(along_z)
        along_y = quarters(dot(wide_y[...], jnp.concatenate([high, low], axis=1)))
        along_y = along_y + jnp.where((kx == 0) & (kz == 0), level * float(POINTS**2), 0.0)
        outer = pltpu.roll(pltpu.roll(along_y, FREQS - 1, 0), FREQS // 2, 1)
        along_y = jnp.where(take_outer, outer, along_y)
        ahead[o, :, k] = along_y.reshape(CHIPS, 8, FREQS)

    def send_ahead(o, first, count):
        def ends(there):
            source = ahead.at[o, there, pl.ds(first, count), pl.ds(0, SENT)]
            return source, arrived.at[pl.ds(place * PLANES + first, count), pl.ds(0, SENT)]

        def send(there):
            source, target = ends(there)
            pltpu.make_async_remote_copy(
                src_ref=source, dst_ref=target,
                send_sem=ahead_send.at[o], recv_sem=ahead_recv.at[0],
                device_id=(band, there * 2 + o), device_id_type=MESH,
            ).start()

        def one(k, _):
            send((chip + k) % CHIPS)
            return 0

        @pl.when(core == o)
        def _():
            source, target = ends(chip)
            pltpu.make_async_copy(source, target, ahead_recv.at[0]).start()

        @pl.when(core != o)
        def _():
            send(chip)

        lax.fori_loop(1, CHIPS, one, 0, unroll=UNROLL)

    def transform(o, first, last):
        def one(k, _):
            forward(o, k)
            return 0

        lax.fori_loop(first, last, one, 0)
        send_ahead(o, first, last - first)


    def middle(o):
        @pl.when(core == o)
        def _():
            landed = arrived.at[:, pl.ds(0, SENT)]
            pltpu.make_async_copy(landed, landed, ahead_recv.at[0]).wait()

            for row in range(SENT):
                column = arrived[:, row, :]
                level = jnp.sum(column, axis=0, keepdims=True) * (1.0 / POINTS)
                high, low = split(column - level)
                along_x = quarters(dot(wide_x[...], jnp.concatenate([high, low], axis=1)))
                along_x = along_x + jnp.where(kx == 0, level * float(POINTS), 0.0)
                high, low = split(along_x * weights[row])
                pair = jnp.concatenate([high, low], axis=1)
                both = dot(tall_x[...], jnp.concatenate([pair, pair], axis=0))
                back[:, row, :] = both[:, :FREQS] + both[:, FREQS:]

    def group(o, h):
        size = PLANES // RETURNS[o]
        return h * size, size

    def give_back(o, h):
        first, size = group(o, h)

        @pl.when(core == o)
        def _():
            def ends(there):
                source = back.at[pl.ds(there * PLANES + first, size), pl.ds(0, SENT)]
                return source, restored.at[o, chip, pl.ds(first, size), pl.ds(0, SENT)]

            def one(k, _):
                there = (place + k) % 32
                source, target = ends(there)
                pltpu.make_async_remote_copy(
                    src_ref=source, dst_ref=target,
                    send_sem=back_send.at[0], recv_sem=back_recv.at[o, h],
                    device_id=(band, there), device_id_type=MESH,
                ).start()
                return 0

            source, target = ends(place)
            pltpu.make_async_copy(source, target, back_recv.at[o, h]).start()
            lax.fori_loop(1, 32, one, 0, unroll=UNROLL)

    def backward(o, k):
        coeffs = restored[o, :, k].reshape(FREQS, FREQS)
        outer = pltpu.roll(pltpu.roll(coeffs, 1, 0), FREQS // 2, 1)
        coeffs = jnp.where(in_disc, jnp.where(row_in == 7, outer, coeffs), 0.0)
        high, low = split(coeffs)
        pair = jnp.concatenate([high, low], axis=1)
        both = dot(tall_y[...], jnp.concatenate([pair, pair], axis=0))
        high, low = split(both[:, :FREQS] + both[:, FREQS:])
        field = dot(jnp.concatenate([high, low], axis=1), jnp.concatenate([wide_ref[:FREQS], wide_ref[:FREQS]], axis=0))
        field = field + dot(high, wide_ref[FREQS:])
        return held[o, plane(o, k)] * field

    for name, *numbers in PROGRAM:
        {"r": relay, "p": pick, "t": transform, "m": middle, "b": give_back}[name](*numbers)

    for h in range(RETURNS[0]):
        first, size = group(0, h)
        part = restored.at[0, :, pl.ds(first, size), pl.ds(0, SENT)]
        pltpu.make_async_copy(part, part, back_recv.at[0, h]).wait()

        def one(k, _):
            partial[plane(0, k)] = backward(0, k)
            return 0

        lax.fori_loop(first, first + size, one, 0)
    for h in range(RETURNS[1]):
        first, size = group(1, h)
        part = restored.at[1, :, pl.ds(first, size), pl.ds(0, SENT)]
        pltpu.make_async_copy(part, part, back_recv.at[1, h]).wait()

        def one(k, _):
            p = plane(1, k)
            out_ref[0, p] = -(partial[p] + backward(1, k))
            return 0

        lax.fori_loop(first, first + size, one, 0)

    for half in range(2):
        part = gathered[half].at[pl.ds(0, 7)]
        pltpu.make_async_copy(part, part, spread_send.at[half]).wait()
    for o in range(2):
        part = held.at[o, pl.ds(0, 7)]
        pltpu.make_async_copy(part, part, tree_send.at[o]).wait()

        @pl.when(core == o)
        def _():
            part = ahead.at[o, pl.ds(0, CHIPS - 1), :, pl.ds(0, SENT)]
            pltpu.make_async_copy(part, part, ahead_send.at[o]).wait()

        @pl.when(core != o)
        def _():
            part = ahead.at[o, :, :, pl.ds(0, SENT)]
            pltpu.make_async_copy(part, part, ahead_send.at[o]).wait()

    part = back.at[pl.ds(0, 31 * PLANES), pl.ds(0, SENT)]
    pltpu.make_async_copy(part, part, back_send.at[0]).wait()


def cas_tables(freqs):
    positions = np.arange(POINTS)[:, None] * freqs[None, :] % POINTS
    angles = positions * (2.0 * math.pi / POINTS)
    cas = np.cos(angles) + np.sin(angles)
    high = cas.astype(ml_dtypes.bfloat16)
    low = (cas - high.astype(np.float64)).astype(ml_dtypes.bfloat16)
    tall = np.concatenate([high, low], axis=1)
    wide = np.concatenate([high.T, low.T], axis=0)
    return tall, wide


def constants():
    tall, wide = cas_tables(np.arange(FREQS) - FREQS // 2)
    ky = []
    for block in range(CHIPS):
        ky += [6 * block + row - 48 for row in range(6)]
        ky += [48 + block, 63 - block] if block < 8 else [-40 - block, block - 71]
    ky[0] = -64
    tall_y, wide_y = cas_tables(np.array(ky))
    tall_x, wide_x = [], []
    for o, band in itertools.product(range(2), range(8)):
        planes = [((band // 2 - r // 2) % 4) * 2 + (band + r) % 2 for r in SCHEMES[o][3]]
        rows = np.concatenate([block * PLANES + np.array(planes) for block in range(POINTS // PLANES)])
        tall_x.append(tall[rows])
        wide_x.append(wide[:, rows])
    return np.stack(tall_x + wide_x + [tall, wide, tall_y, wide_y])


def exchange():
    dma = pltpu.SemaphoreType.DMA
    return pl.pallas_call(
        kernel,
        out_shape=jax.ShapeDtypeStruct((1, PLANES, POINTS, POINTS), F32),
        in_specs=[pl.BlockSpec(memory_space=pl.ANY)] * 3,
        out_specs=pl.BlockSpec(memory_space=pltpu.VMEM),
        scratch_shapes=[
            pltpu.VMEM((POINTS, 2 * FREQS), BF16),
            pltpu.VMEM((2 * FREQS, POINTS), BF16),
            pltpu.VMEM((POINTS, 2 * FREQS), BF16),
            pltpu.VMEM((2 * FREQS, POINTS), BF16),
            pltpu.VMEM((POINTS, 2 * FREQS), BF16),
            pltpu.VMEM((2 * FREQS, POINTS), BF16),
            pltpu.VMEM((8, POINTS // 2, POINTS), F32),
            pltpu.VMEM((8, POINTS // 2, POINTS), F32),
            pltpu.VMEM((2, PLANES, POINTS, POINTS), F32),
            pltpu.VMEM((PLANES, POINTS, POINTS), F32),
            pltpu.VMEM((2, CHIPS, PLANES, 8, FREQS), F32),
            pltpu.VMEM((POINTS, 8, FREQS), F32),
            pltpu.VMEM((POINTS, 8, FREQS), F32),
            pltpu.VMEM((2, CHIPS, PLANES, 8, FREQS), F32),
            pltpu.VMEM((8, FREQS, FREQS), F32),
            pltpu.VMEM((PLANES, POINTS, POINTS), F32),
            pltpu.SMEM((10,), jnp.int32), dma((8,)), pltpu.SemaphoreType.REGULAR((5,)), dma((2,)), dma((2,)), dma((2,)), dma((2, 8, 6)),
            dma((2,)), dma((1,)), dma((1,)), dma((2, max(RETURNS))),
        ],
        compiler_params=pltpu.CompilerParams(
            collective_id=0, has_side_effects=True, vmem_limit_bytes=VMEM_MIB << 20
        ),
    )


def per_device(orbitals, band_ids, owners):
    return exchange()(orbitals, jnp.concatenate([band_ids, owners]), jnp.asarray(constants()))


def solution(mesh):
    placed = (P("band", "fft", None, None), P(), P())
    return jax.shard_map(
        per_device,
        mesh=mesh,
        in_specs=placed,
        out_specs=P("band", "fft", None, None),
        check_vma=False,
    )
```
